32 devices in a mesh: groups: 2 (over x), pool: 16 (over z, y, core).
Axes of the slice: x: 2, y: 2, z: 4, core: 2. Of those that a mesh axis runs over, the one named last changes fastest.
Arguments:
- normed_input_rows: bfloat16 [256, 8192], P(('groups', 'pool')), parts along dimension 0, may hold values from -6 to 6
- gate_base_weight: bfloat16 [8192, 28672], P(None, 'pool'), may hold values from -0.0625 to 0.0625
- adapter_down_factors: bfloat16 [32, 64, 8192], P(('groups', 'pool')), parts along dimension 0, may hold values from -0.0625 to 0.0625
- adapter_up_factors: bfloat16 [32, 64, 28672], P(('groups', 'pool')), parts along dimension 0, may hold values from -0.75 to 0.75
- request_adapter_id: int32 [64, 1], P('groups'), parts along dimension 0, may hold values from 0 to 15; in each aligned block of 32 rows (0 to 31, 32 to 63, ...) at most 3 rows name the same one
- row_request: int32 [256], P('groups'), parts along dimension 0, may hold values from 0 to 31, never falling along the last dimension, each value on 1 to 8 neighbouring positions
- adapter_storage_slot: int32 [32], P('groups'), parts along dimension 0, may hold values from 0 to 15, each once
Outputs:
- gate_out: bfloat16 [256, 28672], P('groups', 'pool'), parts along dimension 0
The draws below stay inside these ranges and needn't reach their ends.
There are 2 independent parts, one for each index of `groups`. The reference program is written for one: setup_inputs(seed, part) draws one part's arguments, and reference() takes and returns one part's arrays. A program takes and returns all parts, laid end to end along the dimension named above; an argument that names none is the same for every part. Nothing has to cross between parts.
Inputs may be any that keep to these rules, and one draw needn't show every extreme that they name: `request_adapter_id`: every adapter serves at least one request and at most 3 requests; some adapter serves exactly 3. `row_request`: rows of one request are consecutive, requests in increasing order, each of 1 to 8 rows. `adapter_storage_slot`: a permutation: each slot holds exactly one adapter; slot s lies on pool index s.
All inputs are finite; a program needn't handle non-finite values.
Results may differ from the reference program's by a relative error of at most 0.004.
Values may be sent and summed in bfloat16 or wider, within the bound.
No kernel may reach another device: no remote copies, remote signals or barrier semaphores. Data moves between devices by JAX's collectives and lax.ppermute only.
A program may use at most 192 MiB of HBM per device.

```python
import math
import jax
import jax.numpy as jnp
import numpy as np
from jax import lax

MODEL_WIDTH = 8192
HIDDEN_UNITS = 28672
ADAPTER_RANK = 64
MOST_REQ = 3
ADAPTER_COUNT = 16
ROWS = 128
REQUESTS = 32


def levels(stream_key, shape, cuts, smallest, high):
    factor_of, own = 1.0, jax.random.fold_in(stream_key, 6)
    for position, shards_of in cuts:
        heights = jnp.exp(jax.random.uniform(jax.random.fold_in(own, position), (shards_of,), jnp.float32, smallest / len(cuts), high / len(cuts)))
        factor_of = factor_of * jnp.repeat(heights, shape[position] // shards_of).reshape([-1 if axis == position else 1 for axis in range(len(shape))])
    return factor_of


def profile(number_of, total, reach, slope):
    weights = [(1 << 20) // math.isqrt(rank ** slope) + 1 for rank in range(2, number_of + 1)]
    rest, holding = total - reach - (number_of - 1), [1] * (number_of - 1)
    while rest > 0:
        candidates = [i for i in range(number_of - 1) if holding[i] < reach]
        pool, remaining = sum([weights[i] for i in candidates]), rest
        for i in candidates:
            more = min(reach - holding[i], max(1, remaining * weights[i] // pool), rest)
            holding[i] = holding[i] + more
            rest = rest - more
    return np.array([reach] + holding)


def ragged(key, count, total, reach, lean):
    if count == 2:
        one = jax.random.randint(key, (), max(1, total - reach), min(reach, total - 1) + 1)
        return jnp.stack([one, total - one])
    sizes = jnp.asarray(profile(count, total, reach, lean), jnp.int32)
    pairs = (count - 1) // 2
    donor, receiver = sizes[1:1 + 2 * pairs:2], sizes[2:2 + 2 * pairs:2]
    room = jnp.minimum(donor - 1, reach - receiver)
    passed = jax.random.randint(jax.random.fold_in(key, 1), (pairs,), 0, 1 << 20) % (room + 1)
    sizes = sizes.at[1:1 + 2 * pairs:2].set(donor - passed).at[2:2 + 2 * pairs:2].set(receiver + passed)
    return sizes[jax.random.permutation(jax.random.fold_in(key, 2), count)]


def deal_out(rng, own, number, rows, count, top, reach, lean):
    sequence = jax.random.permutation(rng, count)
    packed, ordinary = portions_of(count, rows * top, reach, lean, True), portions_of(count, rows * top, reach, lean, False)
    places = jnp.arange(count)

    def named(lengths, rotation):
        used = int((lengths > 0).sum())
        fixed = max(1, used // 4)
        shifted = fixed + (places - fixed + rotation * (used - fixed)) % max(1, count - fixed)
        return jnp.zeros((count,), jnp.int32).at[sequence[jnp.where(places < fixed, places, shifted)]].set(jnp.asarray(lengths, jnp.int32))

    lengths = jnp.where(number % 4 == 0, named(packed, number // 4), named(ordinary, number - number // 4 - 1))
    mixed = jax.random.permutation(jax.random.fold_in(own, 3), count)
    donor, receiver = mixed[0:count // 2 * 2:2], mixed[1:count // 2 * 2:2]
    margin = jnp.minimum(lengths[donor] - 1, reach - lengths[receiver]) // 2
    margin = jnp.where((donor == sequence[0]) | (receiver == sequence[0]) | (lengths[receiver] == 0), 0, jnp.maximum(margin, 0))
    shifted = jax.random.randint(jax.random.fold_in(own, 4), (count // 2,), 0, 1 << 20) % (margin + 1)
    lengths = lengths.at[donor].add(-shifted).at[receiver].add(shifted)
    labels = jnp.searchsorted(jnp.cumsum(lengths), jnp.arange(rows * top), side="right").astype(jnp.int32)
    listing = labels.reshape(top, rows).T
    listing = listing[jax.random.permutation(jax.random.fold_in(own, 1), rows)]
    rotation = jax.random.randint(jax.random.fold_in(own, 2), (rows, 1), 0, top)
    return jnp.take_along_axis(listing, (jnp.arange(top)[None, :] + rotation) % top, axis=1)


def portions_of(number_of, total, most, lean, full):
    portions = [(1 << 20) // math.isqrt(rank ** lean) + 1 for rank in range(1, number_of + 1)]
    largest = most if full else min(most, max(-(-total // number_of), total * portions[0] // sum(portions)))
    least = 1 if total - largest >= number_of - 1 else 0
    given, rest = [largest] + [least] * (number_of - 1), total - largest - least * (number_of - 1)
    while rest > 0:
        free = [i for i in range(1, number_of) if given[i] < largest] or [i for i in range(1, number_of) if given[i] < most]
        pool, left = sum([portions[i] for i in free]), rest
        for i in free:
            more = min(most - given[i], max(1, left * portions[i] // pool), rest)
            given[i] = given[i] + more
            rest = rest - more
    return np.array(given)


def normal_values(key, extent, width, bound, split=(), kind=jnp.bfloat16):
    array = width * jax.random.normal(key, extent, jnp.float32)
    if split:
        array = array * levels(key, extent, split, -0.22, 0.18)
    return jnp.clip(array, -bound, bound).astype(kind)


def setup_inputs(seed: int = 0, part: int = 0) -> dict:
    key_of = jax.random.split(jax.random.key(seed), 8)
    part_splits = jax.random.split(jax.random.fold_in(key_of[7], part), 8)
    normed_input_rows = normal_values(part_splits[0], (ROWS, MODEL_WIDTH), 1.0, 6.0, ((0, 16),))
    gate_base_weight = normal_values(key_of[1], (MODEL_WIDTH, HIDDEN_UNITS), MODEL_WIDTH ** -0.5, 0.0625, ((1, 16),))
    adapter_down_factors = normal_values(part_splits[2], (ADAPTER_COUNT, ADAPTER_RANK, MODEL_WIDTH), MODEL_WIDTH ** -0.5, 0.0625, ((0, 16),))
    adapter_up_factors = normal_values(part_splits[3], (ADAPTER_COUNT, ADAPTER_RANK, HIDDEN_UNITS), ADAPTER_RANK ** -0.5, 0.75, ((0, 16),))
    request_adapter_id_keys = jax.random.split(jax.random.fold_in(part_splits[4], 1), REQUESTS // REQUESTS)
    request_adapter_id_turns = jax.random.permutation(jax.random.fold_in(part_splits[4], 3), REQUESTS // REQUESTS)
    request_adapter_id = jax.vmap(lambda own, number: deal_out(jax.random.fold_in(part_splits[4], 2), own, number, REQUESTS, ADAPTER_COUNT, 1, MOST_REQ, 2))(request_adapter_id_keys, request_adapter_id_turns).reshape((REQUESTS, 1))
    row_request = jnp.searchsorted(jnp.cumsum(ragged(part_splits[5], REQUESTS, ROWS, 8, 2)), jnp.arange(ROWS), side="right").astype(jnp.int32)
    adapter_storage_slot = jax.random.permutation(part_splits[6], ADAPTER_COUNT).astype(jnp.int32)
    return {"normed_input_rows": normed_input_rows, "gate_base_weight": gate_base_weight, "adapter_down_factors": adapter_down_factors, "adapter_up_factors": adapter_up_factors, "request_adapter_id": request_adapter_id, "row_request": row_request, "adapter_storage_slot": adapter_storage_slot}


def reference(normed_input_rows, gate_base_weight, adapter_down_factors, adapter_up_factors, request_adapter_id, row_request, adapter_storage_slot):
    row_slot = adapter_storage_slot[request_adapter_id[row_request, 0]].astype(jnp.int32)
    base = jnp.dot(normed_input_rows, gate_base_weight, preferred_element_type=jnp.float32)

    def shrink_one(pair):
        single_adapter, where_located = pair
        return jnp.dot(adapter_down_factors[where_located], single_adapter, preferred_element_type=jnp.float32)

    low = lax.map(shrink_one, (normed_input_rows, row_slot)).astype(jnp.bfloat16)

    def expand_one(pair):
        rank_vector, where_located = pair
        return jnp.dot(rank_vector, adapter_up_factors[where_located], preferred_element_type=jnp.float32)

    delta = lax.map(expand_one, (low, row_slot))
    return (base + delta).astype(jnp.bfloat16)
```

```python
import jax
import jax.numpy as jnp
from jax import lax
from jax.sharding import PartitionSpec as P

ROW_CAP = 24


def on_device(
    normed_input_rows,
    gate_base_weight,
    adapter_down_factors,
    adapter_up_factors,
    request_adapter_id,
    row_request,
    adapter_storage_slot,
):
    member = lax.axis_index("pool")
    npool = lax.axis_size("pool")
    share, rank = adapter_down_factors.shape[:2]
    adapters = npool * share
    requests = request_adapter_id.shape[0]
    request_slot = jnp.sum(
        jnp.where(
            request_adapter_id == jnp.arange(adapters, dtype=jnp.int32)[None, :],
            adapter_storage_slot[None, :],
            0,
        ),
        axis=1,
    )
    row_slot = jnp.sum(
        jnp.where(
            row_request[:, None] == jnp.arange(requests, dtype=jnp.int32)[None, :],
            request_slot[None, :],
            0,
        ),
        axis=1,
    )
    rows = row_slot.shape[0]
    owner = row_slot // share
    before = jnp.arange(rows)[None, :] < jnp.arange(rows)[:, None]
    place = jnp.sum((before & (owner[:, None] == owner[None, :])).astype(jnp.int32), axis=1)

    x = lax.all_gather(normed_input_rows, "pool", axis=0, tiled=True)
    select = (
        (place[None, :] == jnp.arange(ROW_CAP, dtype=jnp.int32)[:, None])
        & (owner == member)[None, :]
    ).astype(jnp.bfloat16)
    low = jnp.dot(
        x,
        adapter_down_factors.reshape(share * rank, -1).T,
        preferred_element_type=jnp.float32,
    ).astype(jnp.bfloat16)
    which = row_slot - member * share
    mine = which[:, None] == jnp.arange(share * rank, dtype=jnp.int32)[None, :] // rank
    low = jnp.where(mine, low, 0)
    chosen = jnp.dot(select, low, preferred_element_type=jnp.float32).astype(jnp.bfloat16)
    terms = jnp.dot(
        chosen,
        adapter_up_factors.reshape(share * rank, -1),
        preferred_element_type=jnp.float32,
    ).astype(jnp.bfloat16)
    received = lax.all_to_all(terms, "pool", split_axis=1, concat_axis=0, tiled=True)
    base = jnp.dot(x, gate_base_weight, preferred_element_type=jnp.float32)
    base, received = lax.optimization_barrier((base, received))
    pick = (
        (owner * ROW_CAP + place)[:, None]
        == jnp.arange(npool * ROW_CAP, dtype=jnp.int32)[None, :]
    ).astype(jnp.bfloat16)
    delta = jnp.dot(pick, received, preferred_element_type=jnp.float32)
    return (base + delta).astype(jnp.bfloat16)


def solution(mesh):
    in_specs = (
        P(("groups", "pool"), None),
        P(None, "pool"),
        P(("groups", "pool"), None, None),
        P(("groups", "pool"), None, None),
        P("groups", None),
        P("groups"),
        P("groups"),
    )
    out_specs = P("groups", "pool")
    return jax.shard_map(
        on_device, mesh=mesh, in_specs=in_specs, out_specs=out_specs, check_vma=False
    )
```

```python
import jax
import jax.numpy as jnp
from jax import lax
from jax.sharding import PartitionSpec as P

ROW_CAP = 24


def gather(block):
    if lax.axis_size("pool") != 16:
        return lax.all_gather(block, "pool", axis=0, tiled=True), None

    def swap(value, bits):
        return lax.ppermute(value, "pool", [(i, i ^ bits) for i in range(16)])

    far, near, side = swap(block, 8), swap(block, 4), swap(block, 2)
    far_near, far_diagonal = swap(far, 4), swap(far, 6)
    across = swap(jnp.concatenate([near, far]), 2)
    half = jnp.concatenate([block, far, near, side, far_near, far_diagonal, across])
    keys = (0, 8, 4, 2, 12, 14, 6, 10)
    return jnp.concatenate([half, swap(half, 1)]), keys + tuple(k ^ 1 for k in keys)


def on_device(
    normed_input_rows,
    gate_base_weight,
    adapter_down_factors,
    adapter_up_factors,
    request_adapter_id,
    row_request,
    adapter_storage_slot,
):
    member = lax.axis_index("pool")
    npool = lax.axis_size("pool")
    share, rank = adapter_down_factors.shape[:2]
    adapters = npool * share
    requests = request_adapter_id.shape[0]
    request_slot = jnp.sum(
        jnp.where(
            request_adapter_id == jnp.arange(adapters, dtype=jnp.int32)[None, :],
            adapter_storage_slot[None, :],
            0,
        ),
        axis=1,
    )
    row_slot = jnp.sum(
        jnp.where(
            row_request[:, None] == jnp.arange(requests, dtype=jnp.int32)[None, :],
            request_slot[None, :],
            0,
        ),
        axis=1,
    )
    rows = row_slot.shape[0]
    owner = row_slot // share
    before = jnp.arange(rows)[None, :] < jnp.arange(rows)[:, None]
    place = jnp.sum((before & (owner[:, None] == owner[None, :])).astype(jnp.int32), axis=1)

    x, keys = gather(normed_input_rows)
    each = normed_input_rows.shape[0]
    block = jnp.asarray(keys, jnp.int32) ^ member if keys else jnp.arange(npool, dtype=jnp.int32)
    actual = (block[:, None] * each + jnp.arange(each, dtype=jnp.int32)[None, :]).reshape(rows)
    order = actual[:, None] == jnp.arange(rows, dtype=jnp.int32)[None, :]
    slot_here = jnp.sum(jnp.where(order, row_slot[None, :], 0), axis=1)
    place_here = jnp.sum(jnp.where(order, place[None, :], 0), axis=1)
    select = (
        (place_here[None, :] == jnp.arange(ROW_CAP, dtype=jnp.int32)[:, None])
        & (slot_here // share == member)[None, :]
    ).astype(jnp.bfloat16)
    low = jnp.dot(
        x,
        adapter_down_factors.reshape(share * rank, -1).T,
        preferred_element_type=jnp.float32,
    ).astype(jnp.bfloat16)
    which = slot_here - member * share
    mine = which[:, None] == jnp.arange(share * rank, dtype=jnp.int32)[None, :] // rank
    low = jnp.where(mine, low, 0)
    chosen = jnp.dot(select, low, preferred_element_type=jnp.float32).astype(jnp.bfloat16)
    terms = jnp.dot(
        chosen,
        adapter_up_factors.reshape(share * rank, -1),
        preferred_element_type=jnp.float32,
    ).astype(jnp.bfloat16)
    received = lax.all_to_all(terms, "pool", split_axis=1, concat_axis=0, tiled=True)
    if keys:
        x = jnp.dot(
            order.T.astype(jnp.bfloat16), x, preferred_element_type=jnp.float32
        ).astype(jnp.bfloat16)
    base = jnp.dot(x, gate_base_weight, preferred_element_type=jnp.float32)
    base, received = lax.optimization_barrier((base, received))
    pick = (
        (owner * ROW_CAP + place)[:, None]
        == jnp.arange(npool * ROW_CAP, dtype=jnp.int32)[None, :]
    ).astype(jnp.bfloat16)
    delta = jnp.dot(pick, received, preferred_element_type=jnp.float32)
    return (base + delta).astype(jnp.bfloat16)


def solution(mesh):
    in_specs = (
        P(("groups", "pool"), None),
        P(None, "pool"),
        P(("groups", "pool"), None, None),
        P(("groups", "pool"), None, None),
        P("groups", None),
        P("groups"),
        P("groups"),
    )
    out_specs = P("groups", "pool")
    return jax.shard_map(
        on_device, mesh=mesh, in_specs=in_specs, out_specs=out_specs, check_vma=False
    )
```

```python
import jax
import jax.numpy as jnp
from jax import lax
from jax.experimental import pallas as pl
from jax.experimental.pallas import tpu as pltpu
from jax.sharding import PartitionSpec as P

ROW_CAP = 24
CHIP_CAP = 32
CHIP_REST = 2 * ROW_CAP - CHIP_CAP


def slots_and_places(request_adapter_id, row_request, adapter_storage_slot, share):
    adapters = adapter_storage_slot.shape[0]
    requests = request_adapter_id.shape[0]
    request_slot = jnp.sum(
        jnp.where(
            request_adapter_id == jnp.arange(adapters, dtype=jnp.int32)[None, :],
            adapter_storage_slot[None, :],
            0,
        ),
        axis=1,
    )
    row_slot = jnp.sum(
        jnp.where(
            row_request[:, None] == jnp.arange(requests, dtype=jnp.int32)[None, :],
            request_slot[None, :],
            0,
        ),
        axis=1,
    )
    rows = row_slot.shape[0]
    holder = row_slot // share
    before = jnp.arange(rows)[None, :] < jnp.arange(rows)[:, None]
    place = jnp.sum((before & (holder[:, None] == holder[None, :])).astype(jnp.int32), axis=1)
    return row_slot, place


def add_terms(base, received, holder, place, cap):
    at = jnp.where(place < cap, holder * cap + place, -1)
    pick = (at[:, None] == jnp.arange(received.shape[0], dtype=jnp.int32)[None, :]).astype(
        jnp.bfloat16
    )
    return base + jnp.dot(pick, received, preferred_element_type=jnp.float32)


def any_pool(
    normed_input_rows,
    gate_base_weight,
    adapter_down_factors,
    adapter_up_factors,
    request_adapter_id,
    row_request,
    adapter_storage_slot,
):
    member = lax.axis_index("pool")
    share, rank = adapter_down_factors.shape[:2]
    row_slot, place = slots_and_places(
        request_adapter_id, row_request, adapter_storage_slot, share
    )
    owner = row_slot // share
    cap = share * ROW_CAP
    x = lax.all_gather(normed_input_rows, "pool", axis=0, tiled=True)
    select = (
        (place[None, :] == jnp.arange(cap, dtype=jnp.int32)[:, None])
        & (owner == member)[None, :]
    ).astype(jnp.bfloat16)
    low = jnp.dot(
        x,
        adapter_down_factors.reshape(share * rank, -1).T,
        preferred_element_type=jnp.float32,
    ).astype(jnp.bfloat16)
    which = row_slot - member * share
    mine = which[:, None] == jnp.arange(share * rank, dtype=jnp.int32)[None, :] // rank
    low = jnp.where(mine, low, 0)
    chosen = jnp.dot(select, low, preferred_element_type=jnp.float32).astype(jnp.bfloat16)
    terms = jnp.dot(
        chosen,
        adapter_up_factors.reshape(share * rank, -1),
        preferred_element_type=jnp.float32,
    ).astype(jnp.bfloat16)
    received = lax.all_to_all(terms, "pool", split_axis=1, concat_axis=0, tiled=True)
    base = jnp.dot(x, gate_base_weight, preferred_element_type=jnp.float32)
    base, received = lax.optimization_barrier((base, received))
    return add_terms(base, received, owner, place, cap).astype(jnp.bfloat16)


def up_kernel(core, select, low_mine, low_theirs, up_mine, up_theirs, out, mine, theirs):
    rank = up_mine.shape[0]

    @pl.when(pl.program_id(0) == 0)
    def _():
        def pick(which, rows, low):
            return jnp.dot(select[which, rows], low, preferred_element_type=jnp.float32)

        mine[...] = (
            pick(0, 0, low_mine[:, :rank]) + pick(0, 1, low_theirs[:, rank:])
        ).astype(jnp.bfloat16)
        theirs[...] = (
            pick(1, 0, low_mine[:, rank:]) + pick(1, 1, low_theirs[:, :rank])
        ).astype(jnp.bfloat16)

    out[...] = (
        jnp.dot(mine[...], up_mine[...], preferred_element_type=jnp.float32)
        + jnp.dot(theirs[...], up_theirs[...], preferred_element_type=jnp.float32)
    ).astype(jnp.bfloat16)


def up_terms(core, select, low_mine, low_theirs, up_mine, up_theirs, chips, width):
    cap = select.shape[2]
    rank = up_mine.shape[0]

    def whole(shape):
        return pl.BlockSpec(shape, lambda j, core: (0,) * len(shape))

    columns = pl.BlockSpec((rank, width), lambda j, core: (0, 2 * j + core[0]))
    return pl.pallas_call(
        up_kernel,
        grid_spec=pltpu.PrefetchScalarGridSpec(
            num_scalar_prefetch=1,
            grid=(chips,),
            in_specs=[
                whole(select.shape),
                whole(low_mine.shape),
                whole(low_theirs.shape),
                columns,
                columns,
            ],
            out_specs=pl.BlockSpec((cap, width), lambda j, core: (j, 0)),
            scratch_shapes=[pltpu.VMEM((cap, rank), jnp.bfloat16)] * 2,
        ),
        out_shape=jax.ShapeDtypeStruct((chips * cap, width), jnp.bfloat16),
        cost_estimate=pl.CostEstimate(
            flops=4 * cap * rank * chips * width,
            bytes_accessed=4 * rank * chips * width + 2 * cap * chips * width,
            transcendentals=0,
        ),
        name="up_terms",
    )(core, select, low_mine, low_theirs, up_mine, up_theirs)


def chip_pool(
    normed_input_rows,
    gate_base_weight,
    adapter_down_factors,
    adapter_up_factors,
    request_adapter_id,
    row_request,
    adapter_storage_slot,
):
    npool, chips = 16, 8
    member = lax.axis_index("pool")
    core = member & 1
    width = gate_base_weight.shape[1]
    each = normed_input_rows.shape[0]
    rows = row_request.shape[0]

    def swap(value, bits):
        return lax.ppermute(value, "pool", [(i, i ^ bits) for i in range(npool)])

    far = swap(normed_input_rows, 8)
    near = swap(normed_input_rows, 4)
    side = swap(normed_input_rows, 2)
    far_near, far_diagonal = swap(far, 4), swap(far, 6)
    across = swap(jnp.concatenate([near, far]), 2)
    half = jnp.concatenate(
        [normed_input_rows, far, near, side, far_near, far_diagonal, across]
    )
    keys = jnp.asarray((0, 8, 4, 2, 12, 14, 6, 10), jnp.int32)
    down_mine, up_mine = adapter_down_factors[0], adapter_up_factors[0]
    down_theirs, up_theirs = swap(down_mine, 1), swap(up_mine, 1)

    row_slot, place = slots_and_places(
        request_adapter_id, row_request, adapter_storage_slot, 2
    )
    chip = row_slot // 2
    block = jnp.concatenate([keys ^ member, keys ^ member ^ 1])
    actual = (block[:, None] * each + jnp.arange(each, dtype=jnp.int32)[None, :]).reshape(rows)
    order = actual[:, None] == jnp.arange(rows, dtype=jnp.int32)[None, :]
    slot_here = jnp.sum(jnp.where(order, row_slot[None, :], 0), axis=1)
    place_here = jnp.sum(jnp.where(order, place[None, :], 0), axis=1)

    def selection(first, count):
        slots = (member ^ jnp.arange(2, dtype=jnp.int32))[:, None, None, None]
        places = (first + jnp.arange(count, dtype=jnp.int32))[None, None, :, None]
        return (
            (slot_here.reshape(1, 2, 1, -1) == slots)
            & (place_here.reshape(1, 2, 1, -1) == places)
        ).astype(jnp.bfloat16)

    low_mine = jnp.dot(
        half, jnp.concatenate([down_mine, down_theirs]).T, preferred_element_type=jnp.float32
    ).astype(jnp.bfloat16)
    low_theirs = swap(low_mine, 1)
    half, low_theirs = lax.optimization_barrier((half, low_theirs))

    def exchange(first, count):
        terms = up_terms(
            core.reshape(1),
            selection(first, count),
            low_mine,
            low_theirs,
            up_mine,
            up_theirs,
            chips,
            width,
        )
        return lax.all_to_all(
            terms,
            "pool",
            split_axis=0,
            concat_axis=0,
            tiled=True,
            axis_index_groups=[[2 * i + c for i in range(chips)] for c in range(2)],
        )

    received = exchange(0, CHIP_CAP)
    x = jnp.concatenate([half, swap(half, 1)])
    x = jnp.dot(
        order.T.astype(jnp.bfloat16), x, preferred_element_type=jnp.float32
    ).astype(jnp.bfloat16)
    base = jnp.dot(x, gate_base_weight, preferred_element_type=jnp.float32)
    base, received = lax.optimization_barrier((base, received))

    def all_placed(base):
        return add_terms(base, received, chip, place, CHIP_CAP).astype(jnp.bfloat16)

    def some_left(base):
        rest = exchange(CHIP_CAP, CHIP_REST)
        rest_place = jnp.where(place < CHIP_CAP, CHIP_REST, place - CHIP_CAP)
        return all_placed(add_terms(base, rest, chip, rest_place, CHIP_REST))

    return lax.cond(jnp.max(place) < CHIP_CAP, all_placed, some_left, base)


def solution(mesh):
    in_specs = (
        P(("groups", "pool"), None),
        P(None, "pool"),
        P(("groups", "pool"), None, None),
        P(("groups", "pool"), None, None),
        P("groups", None),
        P("groups"),
        P("groups"),
    )
    out_specs = P("groups", "pool")

    def on_device(*blocks):
        width, share = blocks[1].shape[1], blocks[2].shape[0]
        chip_wise = mesh.shape["pool"] == 16 and width % 128 == 0 and share == 1
        return (chip_pool if chip_wise else any_pool)(*blocks)

    return jax.shard_map(
        on_device, mesh=mesh, in_specs=in_specs, out_specs=out_specs, check_vma=False
    )
```

```python
import jax
import jax.numpy as jnp
from jax import lax
from jax.experimental import pallas as pl
from jax.experimental.pallas import tpu as pltpu
from jax.sharding import PartitionSpec as P

ROW_CAP = 24
CHIP_CAP = 32
CHIP_REST = 2 * ROW_CAP - CHIP_CAP


def slots_and_places(request_adapter_id, row_request, adapter_storage_slot, share):
    adapters = adapter_storage_slot.shape[0]
    requests = request_adapter_id.shape[0]
    request_slot = jnp.sum(
        jnp.where(
            request_adapter_id == jnp.arange(adapters, dtype=jnp.int32)[None, :],
            adapter_storage_slot[None, :],
            0,
        ),
        axis=1,
    )
    row_slot = jnp.sum(
        jnp.where(
            row_request[:, None] == jnp.arange(requests, dtype=jnp.int32)[None, :],
            request_slot[None, :],
            0,
        ),
        axis=1,
    )
    rows = row_slot.shape[0]
    holder = row_slot // share
    before = jnp.arange(rows)[None, :] < jnp.arange(rows)[:, None]
    place = jnp.sum((before & (holder[:, None] == holder[None, :])).astype(jnp.int32), axis=1)
    return row_slot, place


def add_terms(base, received, holder, place, cap):
    at = jnp.where(place < cap, holder * cap + place, -1)
    pick = (at[:, None] == jnp.arange(received.shape[0], dtype=jnp.int32)[None, :]).astype(
        jnp.bfloat16
    )
    return base + jnp.dot(pick, received, preferred_element_type=jnp.float32)


def any_pool(
    normed_input_rows,
    gate_base_weight,
    adapter_down_factors,
    adapter_up_factors,
    request_adapter_id,
    row_request,
    adapter_storage_slot,
):
    member = lax.axis_index("pool")
    share, rank = adapter_down_factors.shape[:2]
    row_slot, place = slots_and_places(
        request_adapter_id, row_request, adapter_storage_slot, share
    )
    owner = row_slot // share
    cap = share * ROW_CAP
    x = lax.all_gather(normed_input_rows, "pool", axis=0, tiled=True)
    select = (
        (place[None, :] == jnp.arange(cap, dtype=jnp.int32)[:, None])
        & (owner == member)[None, :]
    ).astype(jnp.bfloat16)
    low = jnp.dot(
        x,
        adapter_down_factors.reshape(share * rank, -1).T,
        preferred_element_type=jnp.float32,
    ).astype(jnp.bfloat16)
    which = row_slot - member * share
    mine = which[:, None] == jnp.arange(share * rank, dtype=jnp.int32)[None, :] // rank
    low = jnp.where(mine, low, 0)
    chosen = jnp.dot(select, low, preferred_element_type=jnp.float32).astype(jnp.bfloat16)
    terms = jnp.dot(
        chosen,
        adapter_up_factors.reshape(share * rank, -1),
        preferred_element_type=jnp.float32,
    ).astype(jnp.bfloat16)
    received = lax.all_to_all(terms, "pool", split_axis=1, concat_axis=0, tiled=True)
    base = jnp.dot(x, gate_base_weight, preferred_element_type=jnp.float32)
    base, received = lax.optimization_barrier((base, received))
    return add_terms(base, received, owner, place, cap).astype(jnp.bfloat16)


KEYS = (0, 8, 4, 2, 12, 14, 6, 10)


def rows_kernel(member, request_id, row_request, slots, select, select_rest, facts, most):
    requests, adapters = request_id.shape[0], slots.shape[1]
    rows = row_request.shape[1]
    me = member[0]

    def iota(shape, axis):
        return lax.broadcasted_iota(jnp.int32, shape, axis)

    def where_sum(mask, values, axis):
        return jnp.sum(jnp.where(mask, values, 0), axis=axis, keepdims=True)

    named = request_id[...] == iota((requests, adapters), 1)
    request_slot = where_sum(named, slots[...], 1)
    asked = row_request[...] == iota((requests, rows), 0)
    slot = where_sum(asked, request_slot, 0)
    down, along = iota((rows, rows), 0), iota((rows, rows), 1)
    slot_down = where_sum(down == along, slot, 1)
    same = (slot_down // 2 == slot // 2) & (down < along)
    place = where_sum(same, jnp.ones((rows, rows), jnp.int32), 0)
    place_down = where_sum(down == along, place, 1)

    lane = iota((1, rows), 1)
    side, lane = lane // (rows // 2), lane % (rows // 2)
    each = rows // (2 * len(KEYS))
    holder = jnp.zeros((1, rows), jnp.int32)
    for i, key in enumerate(KEYS):
        holder = jnp.where(lane // each == i, key, holder)
    actual = ((holder ^ side) ^ me) * each + lane % each
    slot_here = where_sum(down == actual, slot_down, 0)
    place_here = where_sum(down == actual, place_down, 0)
    for first, out in ((0, select), (CHIP_CAP, select_rest)):
        count = out.shape[1]
        placed = place_here == first + iota((count, rows), 0)
        for which in range(2):
            out[which] = jnp.where(placed & (slot_here == (me ^ which)), 1.0, 0.0).astype(
                out.dtype
            )
    line = iota(facts.shape, 0)
    facts[...] = jnp.where(line == 0, slot // 2, jnp.where(line == 1, place, actual))
    most[0] = jnp.max(place)


def row_facts(member, request_adapter_id, row_request, adapter_storage_slot):
    rows = row_request.shape[0]
    smem, vmem = pl.BlockSpec(memory_space=pltpu.SMEM), pl.BlockSpec(memory_space=pltpu.VMEM)
    select, select_rest, facts, most = pl.pallas_call(
        rows_kernel,
        in_specs=[smem, vmem, vmem, vmem],
        out_specs=[vmem, vmem, vmem, smem],
        out_shape=[
            jax.ShapeDtypeStruct((2, CHIP_CAP, rows), jnp.bfloat16),
            jax.ShapeDtypeStruct((2, CHIP_REST, rows), jnp.bfloat16),
            jax.ShapeDtypeStruct((8, rows), jnp.int32),
            jax.ShapeDtypeStruct((1,), jnp.int32),
        ],
        name="row_facts",
    )(
        member.reshape(1),
        request_adapter_id,
        row_request.reshape(1, rows),
        adapter_storage_slot.reshape(1, -1),
    )
    return select, select_rest, facts[0], facts[1], facts[2], most[0]


def low_kernel(
    core, half, down_mine, down_theirs, up_mine, up_theirs, low, columns, sems
):
    rank = up_mine.shape[0]
    chips, _, width = columns.shape

    def copy(j, which, source):
        at = pl.multiple_of((2 * j + core[0]) * width, 128)
        return pltpu.make_async_copy(
            source.at[:, pl.ds(at, width)],
            columns.at[j, pl.ds(which * rank, rank)],
            sems.at[j, which],
        )

    copies = [
        copy(j, which, source)
        for j in range(chips)
        for which, source in enumerate((up_mine, up_theirs))
    ]
    for c in copies:
        c.start()
    total = jnp.zeros(low.shape, jnp.float32)
    depth = half.shape[1] // 8
    for k in range(8):
        part = slice(k * depth, (k + 1) * depth)
        down = jnp.concatenate([down_mine[:, part], down_theirs[:, part]])
        total += lax.dot_general(
            half[:, part], down, (((1,), (1,)), ((), ())), preferred_element_type=jnp.float32
        )
    low[...] = total.astype(low.dtype)
    for c in copies:
        c.wait()


def low_and_columns(core, half, down_mine, down_theirs, up_mine, up_theirs, chips, width):
    rank = up_mine.shape[0]
    vmem, anywhere = pl.BlockSpec(memory_space=pltpu.VMEM), pl.BlockSpec(memory_space=pl.ANY)
    return pl.pallas_call(
        low_kernel,
        in_specs=[
            pl.BlockSpec(memory_space=pltpu.SMEM),
            vmem,
            vmem,
            vmem,
            anywhere,
            anywhere,
        ],
        out_specs=[vmem, vmem],
        out_shape=[
            pltpu.VMEM((half.shape[0], 2 * rank), jnp.bfloat16),
            pltpu.VMEM((chips, 2 * rank, width), jnp.bfloat16),
        ],
        scratch_shapes=[pltpu.SemaphoreType.DMA((chips, 2))],
        compiler_params=pltpu.CompilerParams(vmem_limit_bytes=16 * 2**20),
        cost_estimate=pl.CostEstimate(
            flops=4 * half.size * rank,
            bytes_accessed=4 * rank * chips * width,
            transcendentals=0,
        ),
        name="low_and_columns",
    )(core, half, down_mine, down_theirs, up_mine, up_theirs)


def up_kernel(select, low_mine, low_theirs, columns, out):
    rank = columns.shape[1] // 2
    cap = select.shape[1]
    chosen = []
    for which in range(2):
        here = slice(which * rank, (which + 1) * rank)
        there = slice((1 - which) * rank, (2 - which) * rank)
        low = jnp.concatenate([low_mine[:, here], low_theirs[:, there]])
        chosen.append(jnp.dot(select[which], low, preferred_element_type=jnp.float32))
    low = jnp.concatenate(chosen, axis=1).astype(jnp.bfloat16)
    for j in range(columns.shape[0]):
        out[pl.ds(j * cap, cap), :] = jnp.dot(
            low, columns[j], preferred_element_type=jnp.float32
        ).astype(jnp.bfloat16)


def up_terms(select, low_mine, low_theirs, columns):
    cap = select.shape[1]
    chips, depth, width = columns.shape
    return pl.pallas_call(
        up_kernel,
        in_specs=[pl.BlockSpec(memory_space=pltpu.VMEM)] * 4,
        out_specs=pl.BlockSpec(memory_space=pltpu.VMEM),
        out_shape=jax.ShapeDtypeStruct((chips * cap, width), jnp.bfloat16),
        compiler_params=pltpu.CompilerParams(vmem_limit_bytes=16 * 2**20),
        cost_estimate=pl.CostEstimate(
            flops=2 * cap * depth * chips * width,
            bytes_accessed=2 * (depth + cap) * chips * width,
            transcendentals=0,
        ),
        name="up_terms",
    )(select, low_mine, low_theirs, columns)


def chip_pool(
    normed_input_rows,
    gate_base_weight,
    adapter_down_factors,
    adapter_up_factors,
    request_adapter_id,
    row_request,
    adapter_storage_slot,
):
    npool, chips = 16, 8
    member = lax.axis_index("pool")
    core = member & 1
    width = gate_base_weight.shape[1]
    rows = row_request.shape[0]

    def swap(value, bits):
        return lax.ppermute(value, "pool", [(i, i ^ bits) for i in range(npool)])

    far = swap(normed_input_rows, 8)
    near = swap(normed_input_rows, 4)
    side = swap(normed_input_rows, 2)
    far_near, far_diagonal = swap(far, 4), swap(far, 6)
    across = swap(jnp.concatenate([near, far]), 2)
    half = jnp.concatenate(
        [normed_input_rows, far, near, side, far_near, far_diagonal, across]
    )
    down_mine, up_mine = adapter_down_factors[0], adapter_up_factors[0]
    down_theirs, up_theirs = swap(down_mine, 1), swap(up_mine, 1)

    select, select_rest, chip, place, actual, most = row_facts(
        member, request_adapter_id, row_request, adapter_storage_slot
    )
    half, select, select_rest, chip, place, actual, most = lax.optimization_barrier(
        (half, select, select_rest, chip, place, actual, most)
    )

    def low_here(half):
        return low_and_columns(
            core.reshape(1), half, down_mine, down_theirs, up_mine, up_theirs, chips, width
        )

    low_mine, columns = low_here(half)
    low_theirs = swap(low_mine, 1)
    terms = up_terms(select, low_mine, low_theirs, columns)
    half, terms = lax.optimization_barrier((half, terms))

    def exchange(terms):
        return lax.all_to_all(
            terms,
            "pool",
            split_axis=0,
            concat_axis=0,
            tiled=True,
            axis_index_groups=[[2 * i + c for i in range(chips)] for c in range(2)],
        )

    received = exchange(terms)
    x = jnp.concatenate([half, swap(half, 1)])
    order = (jnp.arange(rows, dtype=jnp.int32)[:, None] == actual[None, :]).astype(jnp.bfloat16)
    x = jnp.dot(order, x, preferred_element_type=jnp.float32).astype(jnp.bfloat16)
    base = jnp.dot(x, gate_base_weight, preferred_element_type=jnp.float32)
    base, received = lax.optimization_barrier((base, received))

    def all_placed(base):
        return add_terms(base, received, chip, place, CHIP_CAP).astype(jnp.bfloat16)

    def some_left(base):
        low_mine, columns = low_here(half)
        rest = exchange(up_terms(select_rest, low_mine, low_theirs, columns))
        rest_place = jnp.where(place < CHIP_CAP, CHIP_REST, place - CHIP_CAP)
        return all_placed(add_terms(base, rest, chip, rest_place, CHIP_REST))

    return lax.cond(most < CHIP_CAP, all_placed, some_left, base)


def solution(mesh):
    in_specs = (
        P(("groups", "pool"), None),
        P(None, "pool"),
        P(("groups", "pool"), None, None),
        P(("groups", "pool"), None, None),
        P("groups", None),
        P("groups"),
        P("groups"),
    )
    out_specs = P("groups", "pool")

    def on_device(*blocks):
        width, share = blocks[1].shape[1], blocks[2].shape[0]
        chip_wise = mesh.shape["pool"] == 16 and width % 128 == 0 and share == 1
        return (chip_pool if chip_wise else any_pool)(*blocks)

    return jax.shard_map(
        on_device, mesh=mesh, in_specs=in_specs, out_specs=out_specs, check_vma=False
    )
```

```python
import functools

import jax
import jax.numpy as jnp
from jax import lax
from jax.experimental import pallas as pl
from jax.experimental.pallas import tpu as pltpu
from jax.sharding import PartitionSpec as P

ROW_CAP = 24
CHIP_CAP = 32
CHIP_REST = 2 * ROW_CAP - CHIP_CAP


def slots_and_places(request_adapter_id, row_request, adapter_storage_slot, share):
    adapters = adapter_storage_slot.shape[0]
    requests = request_adapter_id.shape[0]
    request_slot = jnp.sum(
        jnp.where(
            request_adapter_id == jnp.arange(adapters, dtype=jnp.int32)[None, :],
            adapter_storage_slot[None, :],
            0,
        ),
        axis=1,
    )
    row_slot = jnp.sum(
        jnp.where(
            row_request[:, None] == jnp.arange(requests, dtype=jnp.int32)[None, :],
            request_slot[None, :],
            0,
        ),
        axis=1,
    )
    rows = row_slot.shape[0]
    holder = row_slot // share
    before = jnp.arange(rows)[None, :] < jnp.arange(rows)[:, None]
    place = jnp.sum((before & (holder[:, None] == holder[None, :])).astype(jnp.int32), axis=1)
    return row_slot, place


def add_terms(base, received, holder, place, cap):
    at = jnp.where(place < cap, holder * cap + place, -1)
    pick = (at[:, None] == jnp.arange(received.shape[0], dtype=jnp.int32)[None, :]).astype(
        jnp.bfloat16
    )
    return base + jnp.dot(pick, received, preferred_element_type=jnp.float32)


def any_pool(
    normed_input_rows,
    gate_base_weight,
    adapter_down_factors,
    adapter_up_factors,
    request_adapter_id,
    row_request,
    adapter_storage_slot,
):
    member = lax.axis_index("pool")
    share, rank = adapter_down_factors.shape[:2]
    row_slot, place = slots_and_places(
        request_adapter_id, row_request, adapter_storage_slot, share
    )
    owner = row_slot // share
    cap = share * ROW_CAP
    x = lax.all_gather(normed_input_rows, "pool", axis=0, tiled=True)
    select = (
        (place[None, :] == jnp.arange(cap, dtype=jnp.int32)[:, None])
        & (owner == member)[None, :]
    ).astype(jnp.bfloat16)
    low = jnp.dot(
        x,
        adapter_down_factors.reshape(share * rank, -1).T,
        preferred_element_type=jnp.float32,
    ).astype(jnp.bfloat16)
    which = row_slot - member * share
    mine = which[:, None] == jnp.arange(share * rank, dtype=jnp.int32)[None, :] // rank
    low = jnp.where(mine, low, 0)
    chosen = jnp.dot(select, low, preferred_element_type=jnp.float32).astype(jnp.bfloat16)
    terms = jnp.dot(
        chosen,
        adapter_up_factors.reshape(share * rank, -1),
        preferred_element_type=jnp.float32,
    ).astype(jnp.bfloat16)
    received = lax.all_to_all(terms, "pool", split_axis=1, concat_axis=0, tiled=True)
    base = jnp.dot(x, gate_base_weight, preferred_element_type=jnp.float32)
    base, received = lax.optimization_barrier((base, received))
    return add_terms(base, received, owner, place, cap).astype(jnp.bfloat16)


KEYS = (0, 8, 4, 2, 12, 14, 6, 10)


def start_columns(core, up, outs, sems):
    chips, _, width = outs[0].shape
    copies = []
    for which, out in enumerate(outs):
        for j in range(chips):
            at = pl.multiple_of((2 * j + (core ^ which)) * width, 128)
            copies.append(
                pltpu.make_async_copy(up.at[:, pl.ds(at, width)], out.at[j], sems.at[which, j])
            )
    for c in copies:
        c.start()
    return copies


def columns_kernel(member, up, here, there, sems):
    for c in start_columns(member[0] & 1, up, (here, there), sems):
        c.wait()


def rows_kernel(
    requests,
    member,
    named,
    up,
    select,
    select_rest,
    pick,
    pick_rest,
    order,
    most,
    here,
    there,
    sems,
):
    rows = order.shape[0]
    me = member[0]
    copies = start_columns(me & 1, up, (here, there), sems)
    row_request = named[:, :rows]
    request_id, slots = named[:, rows : rows + requests], named[:, rows + requests :]
    adapters = slots.shape[1]

    def iota(shape, axis):
        return lax.broadcasted_iota(jnp.int32, shape, axis)

    def where_sum(mask, values, axis):
        return jnp.sum(jnp.where(mask, values, 0), axis=axis, keepdims=True)

    def one_hot(mask, out):
        return jnp.where(mask, 1.0, 0.0).astype(out.dtype)

    square = (requests, requests)
    request_down = where_sum(iota(square, 0) == iota(square, 1), request_id, 1)
    request_slot = where_sum(request_down == iota((requests, adapters), 1), slots, 1)
    slot = where_sum(row_request == iota((requests, rows), 0), request_slot, 0)
    down_rows, along = iota((rows, rows), 0), iota((rows, rows), 1)
    slot_down = where_sum(down_rows == along, slot, 1)
    same = (slot_down // 2 == slot // 2) & (down_rows < along)
    place = where_sum(same, jnp.ones((rows, rows), jnp.int32), 0)
    place_down = where_sum(down_rows == along, place, 1)

    lane = iota((1, rows), 1)
    side, lane = lane // (rows // 2), lane % (rows // 2)
    each = rows // (2 * len(KEYS))
    holder = jnp.zeros((1, rows), jnp.int32)
    for i, key in enumerate(KEYS):
        holder = jnp.where(lane // each == i, key, holder)
    actual = ((holder ^ side) ^ me) * each + lane % each
    order[...] = one_hot(down_rows == actual, order)
    slot_here = where_sum(down_rows == actual, slot_down, 0)
    place_here = where_sum(down_rows == actual, place_down, 0)
    for first, choice, back in ((0, select, pick), (CHIP_CAP, select_rest, pick_rest)):
        count = choice.shape[1]
        placed = place_here == first + iota((count, rows), 0)
        for which in range(2):
            choice[which] = one_hot(placed & (slot_here == (me ^ which)), choice)
        at = place_down - first
        at = jnp.where((at >= 0) & (at < count), slot_down // 2 * count + at, -1)
        back[...] = one_hot(at == iota(back.shape, 1), back)
    most[0] = jnp.max(place)
    for c in copies:
        c.wait()


def columns_shapes(up, chips):
    return [pltpu.VMEM((chips, up.shape[0], up.shape[1] // (2 * chips)), jnp.bfloat16)] * 2


def up_columns(member, up, chips):
    vmem = pl.BlockSpec(memory_space=pltpu.VMEM)
    return pl.pallas_call(
        columns_kernel,
        in_specs=[pl.BlockSpec(memory_space=pltpu.SMEM), pl.BlockSpec(memory_space=pl.ANY)],
        out_specs=[vmem] * 2,
        out_shape=columns_shapes(up, chips),
        scratch_shapes=[pltpu.SemaphoreType.DMA((2, chips))],
        compiler_params=pltpu.CompilerParams(vmem_limit_bytes=16 * 2**20),
        name="up_columns",
    )(member.reshape(1), up)


def prepare(member, request_adapter_id, row_request, adapter_storage_slot, up, chips):
    rows = row_request.shape[0]
    smem, vmem = pl.BlockSpec(memory_space=pltpu.SMEM), pl.BlockSpec(memory_space=pltpu.VMEM)
    return pl.pallas_call(
        functools.partial(rows_kernel, request_adapter_id.shape[0]),
        in_specs=[smem, vmem, pl.BlockSpec(memory_space=pl.ANY)],
        out_specs=[vmem] * 5 + [smem] + [vmem] * 2,
        out_shape=[
            pltpu.VMEM((2, CHIP_CAP, rows), jnp.bfloat16),
            jax.ShapeDtypeStruct((2, CHIP_REST, rows), jnp.bfloat16),
            pltpu.VMEM((rows, chips * CHIP_CAP), jnp.bfloat16),
            jax.ShapeDtypeStruct((rows, chips * CHIP_REST), jnp.bfloat16),
            pltpu.VMEM((rows, rows), jnp.bfloat16),
            jax.ShapeDtypeStruct((1,), jnp.int32),
            *columns_shapes(up, chips),
        ],
        scratch_shapes=[pltpu.SemaphoreType.DMA((2, chips))],
        compiler_params=pltpu.CompilerParams(vmem_limit_bytes=16 * 2**20),
        name="prepare",
    )(
        member.reshape(1),
        jnp.concatenate([row_request, request_adapter_id[:, 0], adapter_storage_slot])[None, :],
        up,
    )


def low_kernel(half, down_mine, down_theirs, low):
    total = jnp.zeros(low.shape, jnp.float32)
    depth = half.shape[1] // 8
    for k in range(8):
        part = slice(k * depth, (k + 1) * depth)
        down = jnp.concatenate([down_mine[:, part], down_theirs[:, part]])
        total += lax.dot_general(
            half[:, part], down, (((1,), (1,)), ((), ())), preferred_element_type=jnp.float32
        )
    low[...] = total.astype(low.dtype)


def low_values(half, down_mine, down_theirs):
    rank = down_mine.shape[0]
    vmem = pl.BlockSpec(memory_space=pltpu.VMEM)
    return pl.pallas_call(
        low_kernel,
        in_specs=[vmem] * 3,
        out_specs=vmem,
        out_shape=pltpu.VMEM((half.shape[0], 2 * rank), jnp.bfloat16),
        compiler_params=pltpu.CompilerParams(vmem_limit_bytes=16 * 2**20),
        cost_estimate=pl.CostEstimate(
            flops=4 * half.size * rank, bytes_accessed=2 * half.size, transcendentals=0
        ),
        name="low_values",
    )(half, down_mine, down_theirs)


def up_kernel(select, low_mine, low_theirs, up_mine, up_theirs, out):
    chips, rank, _ = up_mine.shape
    cap = select.shape[1]
    chosen = []
    for which in range(2):
        here = slice(which * rank, (which + 1) * rank)
        there = slice((1 - which) * rank, (2 - which) * rank)
        low = jnp.concatenate([low_mine[:, here], low_theirs[:, there]])
        chosen.append(jnp.dot(select[which], low, preferred_element_type=jnp.float32))
    low = jnp.concatenate(chosen, axis=1).astype(jnp.bfloat16)
    for j in range(chips):
        out[pl.ds(j * cap, cap), :] = jnp.dot(
            low,
            jnp.concatenate([up_mine[j], up_theirs[j]]),
            preferred_element_type=jnp.float32,
        ).astype(jnp.bfloat16)


def up_terms(select, low_mine, low_theirs, up_mine, up_theirs):
    cap = select.shape[1]
    chips, rank, width = up_mine.shape
    vmem = pl.BlockSpec(memory_space=pltpu.VMEM)
    return pl.pallas_call(
        up_kernel,
        in_specs=[vmem] * 5,
        out_specs=vmem,
        out_shape=jax.ShapeDtypeStruct((chips * cap, width), jnp.bfloat16),
        compiler_params=pltpu.CompilerParams(vmem_limit_bytes=16 * 2**20),
        cost_estimate=pl.CostEstimate(
            flops=4 * cap * rank * chips * width,
            bytes_accessed=2 * (2 * rank + cap) * chips * width,
            transcendentals=0,
        ),
        name="up_terms",
    )(select, low_mine, low_theirs, up_mine, up_theirs)


def chip_pool(
    normed_input_rows,
    gate_base_weight,
    adapter_down_factors,
    adapter_up_factors,
    request_adapter_id,
    row_request,
    adapter_storage_slot,
):
    npool, chips = 16, 8
    member = lax.axis_index("pool")

    def swap(value, bits):
        return lax.ppermute(value, "pool", [(i, i ^ bits) for i in range(npool)])

    far = swap(normed_input_rows, 8)
    near = swap(normed_input_rows, 4)
    side = swap(normed_input_rows, 2)
    far_near, far_diagonal = swap(far, 4), swap(far, 6)
    across = swap(jnp.concatenate([near, far]), 2)
    half = jnp.concatenate(
        [normed_input_rows, far, near, side, far_near, far_diagonal, across]
    )
    down, up = adapter_down_factors[0], adapter_up_factors[0]
    down_theirs = swap(down, 1)
    select, select_rest, pick, pick_rest, order, most, up_mine, up_swapped = prepare(
        member, request_adapter_id, row_request, adapter_storage_slot, up, chips
    )
    up_theirs = swap(up_swapped, 1)

    half, up_theirs = lax.optimization_barrier((half, up_theirs))
    low_mine = low_values(half, down, down_theirs)
    low_theirs = swap(low_mine, 1)
    terms = up_terms(select, low_mine, low_theirs, up_mine, up_theirs)
    half, terms = lax.optimization_barrier((half, terms))

    def exchange(terms):
        return lax.all_to_all(
            terms,
            "pool",
            split_axis=0,
            concat_axis=0,
            tiled=True,
            axis_index_groups=[[2 * i + c for i in range(chips)] for c in range(2)],
        )

    received = exchange(terms)
    x = jnp.concatenate([half, swap(half, 1)])
    x = jnp.dot(order, x, preferred_element_type=jnp.float32).astype(jnp.bfloat16)
    base = jnp.dot(x, gate_base_weight, preferred_element_type=jnp.float32)
    base, received = lax.optimization_barrier((base, received))

    def all_placed(base):
        return (base + jnp.dot(pick, received, preferred_element_type=jnp.float32)).astype(
            jnp.bfloat16
        )

    def some_left(base):
        up_mine, up_swapped = up_columns(member, up, chips)
        rest = exchange(
            up_terms(select_rest, low_mine, low_theirs, up_mine, swap(up_swapped, 1))
        )
        return all_placed(
            base + jnp.dot(pick_rest, rest, preferred_element_type=jnp.float32)
        )

    return lax.cond(most[0] < CHIP_CAP, all_placed, some_left, base)


def solution(mesh):
    in_specs = (
        P(("groups", "pool"), None),
        P(None, "pool"),
        P(("groups", "pool"), None, None),
        P(("groups", "pool"), None, None),
        P("groups", None),
        P("groups"),
        P("groups"),
    )
    out_specs = P("groups", "pool")

    def on_device(*blocks):
        width, share = blocks[1].shape[1], blocks[2].shape[0]
        chip_wise = mesh.shape["pool"] == 16 and width % 128 == 0 and share == 1
        return (chip_pool if chip_wise else any_pool)(*blocks)

    return jax.shard_map(
        on_device, mesh=mesh, in_specs=in_specs, out_specs=out_specs, check_vma=False
    )
```

```python
import functools

import jax
import jax.numpy as jnp
from jax import lax
from jax.experimental import pallas as pl
from jax.experimental.pallas import tpu as pltpu
from jax.sharding import PartitionSpec as P

ROW_CAP = 24
CHIP_CAPS = (24, 28, 32)
CHIP_CAP = CHIP_CAPS[-1]
CHIP_REST = 2 * ROW_CAP - CHIP_CAP
PIECE = 8


def slots_and_places(request_adapter_id, row_request, adapter_storage_slot, share):
    adapters = adapter_storage_slot.shape[0]
    requests = request_adapter_id.shape[0]
    request_slot = jnp.sum(
        jnp.where(
            request_adapter_id == jnp.arange(adapters, dtype=jnp.int32)[None, :],
            adapter_storage_slot[None, :],
            0,
        ),
        axis=1,
    )
    row_slot = jnp.sum(
        jnp.where(
            row_request[:, None] == jnp.arange(requests, dtype=jnp.int32)[None, :],
            request_slot[None, :],
            0,
        ),
        axis=1,
    )
    rows = row_slot.shape[0]
    holder = row_slot // share
    before = jnp.arange(rows)[None, :] < jnp.arange(rows)[:, None]
    place = jnp.sum((before & (holder[:, None] == holder[None, :])).astype(jnp.int32), axis=1)
    return row_slot, place


def add_terms(base, received, holder, place, cap):
    at = jnp.where(place < cap, holder * cap + place, -1)
    pick = (at[:, None] == jnp.arange(received.shape[0], dtype=jnp.int32)[None, :]).astype(
        jnp.bfloat16
    )
    return base + jnp.dot(pick, received, preferred_element_type=jnp.float32)


def any_pool(
    normed_input_rows,
    gate_base_weight,
    adapter_down_factors,
    adapter_up_factors,
    request_adapter_id,
    row_request,
    adapter_storage_slot,
):
    member = lax.axis_index("pool")
    share, rank = adapter_down_factors.shape[:2]
    row_slot, place = slots_and_places(
        request_adapter_id, row_request, adapter_storage_slot, share
    )
    owner = row_slot // share
    cap = share * ROW_CAP
    x = lax.all_gather(normed_input_rows, "pool", axis=0, tiled=True)
    select = (
        (place[None, :] == jnp.arange(cap, dtype=jnp.int32)[:, None])
        & (owner == member)[None, :]
    ).astype(jnp.bfloat16)
    low = jnp.dot(
        x,
        adapter_down_factors.reshape(share * rank, -1).T,
        preferred_element_type=jnp.float32,
    ).astype(jnp.bfloat16)
    which = row_slot - member * share
    mine = which[:, None] == jnp.arange(share * rank, dtype=jnp.int32)[None, :] // rank
    low = jnp.where(mine, low, 0)
    chosen = jnp.dot(select, low, preferred_element_type=jnp.float32).astype(jnp.bfloat16)
    terms = jnp.dot(
        chosen,
        adapter_up_factors.reshape(share * rank, -1),
        preferred_element_type=jnp.float32,
    ).astype(jnp.bfloat16)
    received = lax.all_to_all(terms, "pool", split_axis=1, concat_axis=0, tiled=True)
    base = jnp.dot(x, gate_base_weight, preferred_element_type=jnp.float32)
    base, received = lax.optimization_barrier((base, received))
    return add_terms(base, received, owner, place, cap).astype(jnp.bfloat16)


KEYS = (0, 8, 4, 2, 12, 14, 6, 10)


def start_columns(core, up, outs, sems):
    chips, _, width = outs[0].shape
    copies = []
    for which, out in enumerate(outs):
        for j in range(chips):
            at = pl.multiple_of((2 * j + (core ^ which)) * width, 128)
            copies.append(
                pltpu.make_async_copy(up.at[:, pl.ds(at, width)], out.at[j], sems.at[which, j])
            )
    for c in copies:
        c.start()
    return copies


def columns_kernel(member, up, here, there, sems):
    for c in start_columns(member[0] & 1, up, (here, there), sems):
        c.wait()


def iota(shape, axis):
    return lax.broadcasted_iota(jnp.int32, shape, axis)


def where_sum(mask, values, axis):
    return jnp.sum(jnp.where(mask, values, 0), axis=axis, keepdims=True)


def one_hot(mask, out):
    return jnp.where(mask, 1.0, 0.0).astype(out.dtype)


def rows_and_places(me, rows, requests, named):
    row_request = named[:, :rows]
    request_id, slots = named[:, rows : rows + requests], named[:, rows + requests :]
    adapters = slots.shape[1]
    square = (requests, requests)
    request_down = where_sum(iota(square, 0) == iota(square, 1), request_id, 1)
    request_slot = where_sum(request_down == iota((requests, adapters), 1), slots, 1)
    slot = where_sum(row_request == iota((requests, rows), 0), request_slot, 0)
    down, along = iota((rows, rows), 0), iota((rows, rows), 1)
    slot_down = where_sum(down == along, slot, 1)
    same = slot_down // 2 == slot // 2
    place = where_sum(same & (down < along), jnp.ones((rows, rows), jnp.int32), 0)
    place_down = where_sum(same & (along < down), jnp.ones((rows, rows), jnp.int32), 1)

    lane = iota((1, rows), 1)
    side, lane = lane // (rows // 2), lane % (rows // 2)
    each = rows // (2 * len(KEYS))
    holder = jnp.zeros((1, rows), jnp.int32)
    for i, key in enumerate(KEYS):
        holder = jnp.where(lane // each == i, key, holder)
    actual = ((holder ^ side) ^ me) * each + lane % each
    return place, slot_down, place_down, actual, down


def rows_kernel(requests, member, named, up, select, select_rest, way, here, there, sems):
    rows = select.shape[2]
    me = member[0]
    copies = start_columns(me & 1, up, (here, there), sems)
    place, slot_down, place_down, actual, down = rows_and_places(me, rows, requests, named)
    both = where_sum(down == actual, slot_down * rows + place_down, 0)
    slot_here, place_here = both // rows, both % rows
    for first, choice in ((0, select), (CHIP_CAP, select_rest)):
        count = choice.shape[1]
        placed = place_here == first + iota((count, rows), 0)
        for which in range(2):
            choice[which] = one_hot(placed & (slot_here == (me ^ which)), choice)
    most = jnp.max(place)
    way[0] = sum((most >= cap).astype(jnp.int32) for cap in CHIP_CAPS)
    for c in copies:
        c.wait()


def picks_kernel(requests, member, named, pick, pick_rest, pick_right, order):
    rows = order.shape[0]
    _, slot_down, place_down, actual, down = rows_and_places(member[0], rows, requests, named)
    order[...] = one_hot(down == actual, order)
    line = pick_right.shape[1]
    for first, count, back in ((0, CHIP_CAP, pick), (CHIP_CAP, CHIP_REST, pick_rest)):
        at = place_down - first
        in_piece = slot_down // 2 * PIECE + at % PIECE
        at = jnp.where((at >= 0) & (at < count), at // PIECE * line + in_piece, -1)
        back[...] = one_hot(at == iota(back.shape, 1), back)
    at = place_down % PIECE + PIECE // 2
    at = jnp.where((place_down // PIECE == 3) & (at < PIECE), slot_down // 2 * PIECE + at, -1)
    pick_right[...] = one_hot(at == iota(pick_right.shape, 1), pick_right)


def columns_shapes(up, chips):
    return [pltpu.VMEM((chips, up.shape[0], up.shape[1] // (2 * chips)), jnp.bfloat16)] * 2


def up_columns(member, up, chips):
    vmem = pl.BlockSpec(memory_space=pltpu.VMEM)
    return pl.pallas_call(
        columns_kernel,
        in_specs=[pl.BlockSpec(memory_space=pltpu.SMEM), pl.BlockSpec(memory_space=pl.ANY)],
        out_specs=[vmem] * 2,
        out_shape=columns_shapes(up, chips),
        scratch_shapes=[pltpu.SemaphoreType.DMA((2, chips))],
        compiler_params=pltpu.CompilerParams(vmem_limit_bytes=16 * 2**20),
        name="up_columns",
    )(member.reshape(1), up)


def prepare(member, requests, named, up, chips, rows):
    smem, vmem = pl.BlockSpec(memory_space=pltpu.SMEM), pl.BlockSpec(memory_space=pltpu.VMEM)
    return pl.pallas_call(
        functools.partial(rows_kernel, requests),
        in_specs=[smem, vmem, pl.BlockSpec(memory_space=pl.ANY)],
        out_specs=[vmem] * 2 + [smem] + [vmem] * 2,
        out_shape=[
            pltpu.VMEM((2, CHIP_CAP, rows), jnp.bfloat16),
            jax.ShapeDtypeStruct((2, CHIP_REST, rows), jnp.bfloat16),
            jax.ShapeDtypeStruct((1,), jnp.int32),
            *columns_shapes(up, chips),
        ],
        scratch_shapes=[pltpu.SemaphoreType.DMA((2, chips))],
        compiler_params=pltpu.CompilerParams(vmem_limit_bytes=16 * 2**20),
        name="prepare",
    )(member.reshape(1), named, up)


def picks(member, requests, named, chips, rows):
    vmem = pl.BlockSpec(memory_space=pltpu.VMEM)
    widths = (chips * CHIP_CAP, chips * CHIP_REST, chips * PIECE, rows)
    return pl.pallas_call(
        functools.partial(picks_kernel, requests),
        in_specs=[pl.BlockSpec(memory_space=pltpu.SMEM), vmem],
        out_specs=[vmem] * 4,
        out_shape=[jax.ShapeDtypeStruct((rows, width), jnp.bfloat16) for width in widths],
        name="picks",
    )(member.reshape(1), named)


def low_kernel(half, down_mine, down_theirs, low):
    total = jnp.zeros(low.shape, jnp.float32)
    depth = half.shape[1] // 8
    for k in range(8):
        part = slice(k * depth, (k + 1) * depth)
        down = jnp.concatenate([down_mine[:, part], down_theirs[:, part]])
        total += lax.dot_general(
            half[:, part], down, (((1,), (1,)), ((), ())), preferred_element_type=jnp.float32
        )
    low[...] = total.astype(low.dtype)


def low_values(half, down_mine, down_theirs):
    rank = down_mine.shape[0]
    vmem = pl.BlockSpec(memory_space=pltpu.VMEM)
    return pl.pallas_call(
        low_kernel,
        in_specs=[vmem] * 3,
        out_specs=vmem,
        out_shape=pltpu.VMEM((half.shape[0], 2 * rank), jnp.bfloat16),
        compiler_params=pltpu.CompilerParams(vmem_limit_bytes=16 * 2**20),
        cost_estimate=pl.CostEstimate(
            flops=4 * half.size * rank, bytes_accessed=2 * half.size, transcendentals=0
        ),
        name="low_values",
    )(half, down_mine, down_theirs)


def up_kernel(caps, way, select, low_mine, low_theirs, up_mine, up_theirs, *refs):
    outs = refs
    chips, rank, width = up_mine.shape
    taken = [way[0] == k for k in range(len(caps) - 1)] + [way[0] >= len(caps) - 1]

    chosen = []
    for which in range(2):
        here = slice(which * rank, (which + 1) * rank)
        there = slice((1 - which) * rank, (2 - which) * rank)
        low = jnp.concatenate([low_mine[:, here], low_theirs[:, there]])
        chosen.append(jnp.dot(select[which], low, preferred_element_type=jnp.float32))
    low = jnp.concatenate(chosen, axis=1).astype(jnp.bfloat16)
    for k, cap in enumerate(caps):

        @pl.when(taken[k])
        def _():
            for j in range(chips):
                terms = jnp.dot(
                    low,
                    jnp.concatenate([up_mine[j], up_theirs[j]]),
                    preferred_element_type=jnp.float32,
                )
                for i in range(cap // PIECE):
                    outs[k][j, :, i * width : (i + 1) * width] = terms[
                        i * PIECE : (i + 1) * PIECE
                    ].astype(outs[k].dtype)
                if cap % PIECE:
                    i = cap // PIECE
                    last = terms[i * PIECE : cap]
                    outs[k][j, :, i * width :] = jnp.concatenate(
                        [last[:, : width // 2], last[:, width // 2 :]]
                    ).astype(outs[k].dtype)


def up_terms(caps, way, select, low_mine, low_theirs, up_mine, up_theirs):
    chips, rank, width = up_mine.shape
    vmem = pl.BlockSpec(memory_space=pltpu.VMEM)
    shapes = [(chips, PIECE, cap * width // PIECE) for cap in caps]
    return pl.pallas_call(
        functools.partial(up_kernel, caps),
        in_specs=[pl.BlockSpec(memory_space=pltpu.SMEM)] + [vmem] * 5,
        out_specs=[vmem] * len(caps),
        out_shape=[pltpu.VMEM(shape, jnp.bfloat16) for shape in shapes],
        compiler_params=pltpu.CompilerParams(vmem_limit_bytes=16 * 2**20),
        cost_estimate=pl.CostEstimate(
            flops=4 * caps[-1] * rank * chips * width,
            bytes_accessed=2 * (2 * rank + caps[-1]) * chips * width,
            transcendentals=0,
        ),
        name="up_terms",
    )(way, select, low_mine, low_theirs, up_mine, up_theirs)


def add_kernel(base, received, pick, pick_right, out):
    rows, width = base.shape
    line, total = received.shape
    whole, part = total // width, total % width
    step = width // 2
    for half in range(2):
        columns = slice(half * step, (half + 1) * step)
        value = base[:, columns]
        for i in range(whole):
            piece = received[:, i * width + half * step : i * width + (half + 1) * step]
            value += jnp.dot(
                pick[:, i * line : (i + 1) * line], piece, preferred_element_type=jnp.float32
            )
        if part:
            choice = pick_right[...] if half else pick[:, whole * line : (whole + 1) * line]
            value += jnp.dot(
                choice, received[:, whole * width :], preferred_element_type=jnp.float32
            )
        out[:, columns] = value.astype(out.dtype)


def add_received(base, received, pick, pick_right, dtype):
    rows, width = base.shape
    vmem = pl.BlockSpec(memory_space=pltpu.VMEM)
    return pl.pallas_call(
        add_kernel,
        in_specs=[vmem] * 4,
        out_specs=vmem,
        out_shape=jax.ShapeDtypeStruct((rows, width), dtype),
        compiler_params=pltpu.CompilerParams(vmem_limit_bytes=24 * 2**20),
        cost_estimate=pl.CostEstimate(
            flops=4 * pick.size * width, bytes_accessed=8 * rows * width, transcendentals=0
        ),
        name="add_received",
    )(base, received.reshape(-1, received.shape[2]), pick, pick_right)


def chip_pool(
    normed_input_rows,
    gate_base_weight,
    adapter_down_factors,
    adapter_up_factors,
    request_adapter_id,
    row_request,
    adapter_storage_slot,
):
    npool, chips = 16, 8
    member = lax.axis_index("pool")

    def swap(value, bits):
        return lax.ppermute(value, "pool", [(i, i ^ bits) for i in range(npool)])

    far = swap(normed_input_rows, 8)
    near = swap(normed_input_rows, 4)
    side = swap(normed_input_rows, 2)
    far_near, far_diagonal = swap(far, 4), swap(far, 6)
    across = swap(jnp.concatenate([near, far]), 2)
    half = jnp.concatenate(
        [normed_input_rows, far, near, side, far_near, far_diagonal, across]
    )
    down, up = adapter_down_factors[0], adapter_up_factors[0]
    down_theirs = swap(down, 1)
    requests, rows = request_adapter_id.shape[0], row_request.shape[0]
    named = jnp.concatenate([row_request, request_adapter_id[:, 0], adapter_storage_slot])[None, :]
    select, select_rest, way, up_mine, up_swapped = prepare(
        member, requests, named, up, chips, rows
    )
    up_theirs = swap(up_swapped, 1)

    half, up_theirs = lax.optimization_barrier((half, up_theirs))
    low_mine = low_values(half, down, down_theirs)
    low_theirs = swap(low_mine, 1)

    def exchange(terms):
        return lax.all_to_all(
            terms,
            "pool",
            split_axis=0,
            concat_axis=0,
            tiled=True,
            axis_index_groups=[[2 * i + c for i in range(chips)] for c in range(2)],
        )

    terms = up_terms(CHIP_CAPS, way, select, low_mine, low_theirs, up_mine, up_theirs)
    half, *terms = lax.optimization_barrier((half, *terms))

    def finish(k, some_left, half):
        received = exchange(terms[k])
        swapped, named_then = lax.optimization_barrier((swap(half, 1), named))
        pick, pick_rest, pick_right, order = picks(member, requests, named_then, chips, rows)
        x = jnp.concatenate([half, swapped])
        x = jnp.dot(order, x, preferred_element_type=jnp.float32).astype(jnp.bfloat16)
        base = jnp.dot(x, gate_base_weight, preferred_element_type=jnp.float32)
        base, received = lax.optimization_barrier((base, received))
        if some_left:
            up_here, up_there = up_columns(member, up, chips)
            (rest,) = up_terms(
                (CHIP_REST,), way, select_rest, low_mine, low_theirs, up_here, swap(up_there, 1)
            )
            rest = exchange(rest)
            base = add_received(base, rest, pick_rest, pick_right, jnp.float32)
        return add_received(base, received, pick, pick_right, jnp.bfloat16)

    last = len(CHIP_CAPS) - 1
    ways = [functools.partial(finish, k, False) for k in range(last + 1)]
    ways.append(functools.partial(finish, last, True))
    return lax.switch(way[0], ways, half)


def solution(mesh):
    in_specs = (
        P(("groups", "pool"), None),
        P(None, "pool"),
        P(("groups", "pool"), None, None),
        P(("groups", "pool"), None, None),
        P("groups", None),
        P("groups"),
        P("groups"),
    )
    out_specs = P("groups", "pool")

    def on_device(*blocks):
        width, share = blocks[1].shape[1], blocks[2].shape[0]
        chip_wise = mesh.shape["pool"] == 16 and width % 128 == 0 and share == 1
        return (chip_pool if chip_wise else any_pool)(*blocks)

    return jax.shard_map(
        on_device, mesh=mesh, in_specs=in_specs, out_specs=out_specs, check_vma=False
    )
```

```python
import functools

import jax
import jax.numpy as jnp
from jax import lax
from jax.experimental import pallas as pl
from jax.experimental.pallas import tpu as pltpu
from jax.sharding import PartitionSpec as P

ROW_CAP = 24
CHIP_CAPS = (24, 28, 32, 2 * ROW_CAP)
PIECE = 8


def slots_and_places(request_adapter_id, row_request, adapter_storage_slot, share):
    adapters = adapter_storage_slot.shape[0]
    requests = request_adapter_id.shape[0]
    request_slot = jnp.sum(
        jnp.where(
            request_adapter_id == jnp.arange(adapters, dtype=jnp.int32)[None, :],
            adapter_storage_slot[None, :],
            0,
        ),
        axis=1,
    )
    row_slot = jnp.sum(
        jnp.where(
            row_request[:, None] == jnp.arange(requests, dtype=jnp.int32)[None, :],
            request_slot[None, :],
            0,
        ),
        axis=1,
    )
    rows = row_slot.shape[0]
    holder = row_slot // share
    before = jnp.arange(rows)[None, :] < jnp.arange(rows)[:, None]
    place = jnp.sum((before & (holder[:, None] == holder[None, :])).astype(jnp.int32), axis=1)
    return row_slot, place


def add_terms(base, received, holder, place, cap):
    at = jnp.where(place < cap, holder * cap + place, -1)
    pick = (at[:, None] == jnp.arange(received.shape[0], dtype=jnp.int32)[None, :]).astype(
        jnp.bfloat16
    )
    return base + jnp.dot(pick, received, preferred_element_type=jnp.float32)


def any_pool(
    normed_input_rows,
    gate_base_weight,
    adapter_down_factors,
    adapter_up_factors,
    request_adapter_id,
    row_request,
    adapter_storage_slot,
):
    member = lax.axis_index("pool")
    share, rank = adapter_down_factors.shape[:2]
    row_slot, place = slots_and_places(
        request_adapter_id, row_request, adapter_storage_slot, share
    )
    owner = row_slot // share
    cap = share * ROW_CAP
    x = lax.all_gather(normed_input_rows, "pool", axis=0, tiled=True)
    select = (
        (place[None, :] == jnp.arange(cap, dtype=jnp.int32)[:, None])
        & (owner == member)[None, :]
    ).astype(jnp.bfloat16)
    low = jnp.dot(
        x,
        adapter_down_factors.reshape(share * rank, -1).T,
        preferred_element_type=jnp.float32,
    ).astype(jnp.bfloat16)
    which = row_slot - member * share
    mine = which[:, None] == jnp.arange(share * rank, dtype=jnp.int32)[None, :] // rank
    low = jnp.where(mine, low, 0)
    chosen = jnp.dot(select, low, preferred_element_type=jnp.float32).astype(jnp.bfloat16)
    terms = jnp.dot(
        chosen,
        adapter_up_factors.reshape(share * rank, -1),
        preferred_element_type=jnp.float32,
    ).astype(jnp.bfloat16)
    received = lax.all_to_all(terms, "pool", split_axis=1, concat_axis=0, tiled=True)
    base = jnp.dot(x, gate_base_weight, preferred_element_type=jnp.float32)
    base, received = lax.optimization_barrier((base, received))
    return add_terms(base, received, owner, place, cap).astype(jnp.bfloat16)


KEYS = (0, 8, 4, 2, 12, 14, 6, 10)


def start_columns(core, up, outs, sems):
    chips, _, width = outs[0].shape
    copies = []
    for which, out in enumerate(outs):
        for j in range(chips):
            at = pl.multiple_of((2 * j + (core ^ which)) * width, 128)
            copies.append(
                pltpu.make_async_copy(up.at[:, pl.ds(at, width)], out.at[j], sems.at[which, j])
            )
    for c in copies:
        c.start()
    return copies


def iota(shape, axis):
    return lax.broadcasted_iota(jnp.int32, shape, axis)


def where_sum(mask, values, axis):
    return jnp.sum(jnp.where(mask, values, 0), axis=axis, keepdims=True)


def one_hot(mask, out):
    return jnp.where(mask, 1.0, 0.0).astype(out.dtype)


def rows_and_places(me, rows, requests, named):
    row_request = named[:, :rows]
    request_id, slots = named[:, rows : rows + requests], named[:, rows + requests :]
    adapters = slots.shape[1]
    square = (requests, requests)
    request_down = where_sum(iota(square, 0) == iota(square, 1), request_id, 1)
    request_slot = where_sum(request_down == iota((requests, adapters), 1), slots, 1)
    slot = where_sum(row_request == iota((requests, rows), 0), request_slot, 0)
    down, along = iota((rows, rows), 0), iota((rows, rows), 1)
    slot_down = where_sum(down == along, slot, 1)
    same = slot_down // 2 == slot // 2
    place = where_sum(same & (down < along), jnp.ones((rows, rows), jnp.int32), 0)
    place_down = where_sum(same & (along < down), jnp.ones((rows, rows), jnp.int32), 1)

    lane = iota((1, rows), 1)
    side, lane = lane // (rows // 2), lane % (rows // 2)
    each = rows // (2 * len(KEYS))
    holder = jnp.zeros((1, rows), jnp.int32)
    for i, key in enumerate(KEYS):
        holder = jnp.where(lane // each == i, key, holder)
    actual = ((holder ^ side) ^ me) * each + lane % each
    return place, slot_down, place_down, actual, down


def rows_kernel(requests, member, named, up, select, way, here, there, sems):
    rows = select.shape[2]
    me = member[0]
    copies = start_columns(me & 1, up, (here, there), sems)
    place, slot_down, place_down, actual, down = rows_and_places(me, rows, requests, named)
    both = where_sum(down == actual, slot_down * rows + place_down, 0)
    slot_here, place_here = both // rows, both % rows
    placed = place_here == iota(select.shape[1:], 0)
    for which in range(2):
        select[which] = one_hot(placed & (slot_here == (me ^ which)), select)
    most = jnp.max(place)
    way[0] = sum((most >= cap).astype(jnp.int32) for cap in CHIP_CAPS[:-1])
    for c in copies:
        c.wait()


def picks_kernel(requests, member, named, pick, pick_right, order):
    rows = order.shape[0]
    _, slot_down, place_down, actual, down = rows_and_places(member[0], rows, requests, named)
    order[...] = one_hot(down == actual, order)
    line = pick_right.shape[1]
    at = place_down // PIECE * line + slot_down // 2 * PIECE + place_down % PIECE
    pick[...] = one_hot(at == iota(pick.shape, 1), pick)
    at = place_down % PIECE + PIECE // 2
    at = jnp.where((place_down // PIECE == 3) & (at < PIECE), slot_down // 2 * PIECE + at, -1)
    pick_right[...] = one_hot(at == iota(pick_right.shape, 1), pick_right)


def columns_shapes(up, chips):
    return [pltpu.VMEM((chips, up.shape[0], up.shape[1] // (2 * chips)), jnp.bfloat16)] * 2


def prepare(member, requests, named, up, chips, rows):
    smem, vmem = pl.BlockSpec(memory_space=pltpu.SMEM), pl.BlockSpec(memory_space=pltpu.VMEM)
    return pl.pallas_call(
        functools.partial(rows_kernel, requests),
        in_specs=[smem, vmem, pl.BlockSpec(memory_space=pl.ANY)],
        out_specs=[vmem, smem, vmem, vmem],
        out_shape=[
            pltpu.VMEM((2, CHIP_CAPS[-1], rows), jnp.bfloat16),
            jax.ShapeDtypeStruct((1,), jnp.int32),
            *columns_shapes(up, chips),
        ],
        scratch_shapes=[pltpu.SemaphoreType.DMA((2, chips))],
        compiler_params=pltpu.CompilerParams(vmem_limit_bytes=16 * 2**20),
        name="prepare",
    )(member.reshape(1), named, pltpu.with_memory_space_constraint(up, pltpu.HBM))


def picks(member, requests, named, chips, rows):
    vmem = pl.BlockSpec(memory_space=pltpu.VMEM)
    widths = (chips * CHIP_CAPS[-1], chips * PIECE, rows)
    return pl.pallas_call(
        functools.partial(picks_kernel, requests),
        in_specs=[pl.BlockSpec(memory_space=pltpu.SMEM), vmem],
        out_specs=[vmem] * 3,
        out_shape=[jax.ShapeDtypeStruct((rows, width), jnp.bfloat16) for width in widths],
        name="picks",
    )(member.reshape(1), named)


def low_kernel(half, down_mine, down_theirs, low):
    total = jnp.zeros(low.shape, jnp.float32)
    depth = half.shape[1] // 8
    for k in range(8):
        part = slice(k * depth, (k + 1) * depth)
        down = jnp.concatenate([down_mine[:, part], down_theirs[:, part]])
        total += lax.dot_general(
            half[:, part], down, (((1,), (1,)), ((), ())), preferred_element_type=jnp.float32
        )
    low[...] = total.astype(low.dtype)


def low_values(half, down_mine, down_theirs):
    rank = down_mine.shape[0]
    vmem = pl.BlockSpec(memory_space=pltpu.VMEM)
    return pl.pallas_call(
        low_kernel,
        in_specs=[vmem] * 3,
        out_specs=vmem,
        out_shape=pltpu.VMEM((half.shape[0], 2 * rank), jnp.bfloat16),
        compiler_params=pltpu.CompilerParams(vmem_limit_bytes=16 * 2**20),
        cost_estimate=pl.CostEstimate(
            flops=4 * half.size * rank, bytes_accessed=2 * half.size, transcendentals=0
        ),
        name="low_values",
    )(half, down_mine, down_theirs)


def up_kernel(caps, way, select, low_mine, low_theirs, up_mine, up_theirs, *refs):
    outs, staged, sems = refs[: len(caps)], refs[-2], refs[-1]
    chips, rank, width = up_mine.shape
    taken = [way[0] == k for k in range(len(caps))]

    chosen = []
    for which in range(2):
        here = slice(which * rank, (which + 1) * rank)
        there = slice((1 - which) * rank, (2 - which) * rank)
        low = jnp.concatenate([low_mine[:, here], low_theirs[:, there]])
        chosen.append(jnp.dot(select[which], low, preferred_element_type=jnp.float32))
    low = jnp.concatenate(chosen, axis=1).astype(jnp.bfloat16)
    for k, cap in enumerate(caps):

        @pl.when(taken[k])
        def _():
            kept = low[: max(cap, caps[-2])]
            copies = []
            for j in range(chips):
                terms = jnp.dot(
                    kept,
                    jnp.concatenate([up_mine[j], up_theirs[j]]),
                    preferred_element_type=jnp.float32,
                )
                for i in range(cap // PIECE):
                    staged[j, :, i * width : (i + 1) * width] = terms[
                        i * PIECE : (i + 1) * PIECE
                    ].astype(staged.dtype)
                end = cap * width // PIECE
                if cap % PIECE:
                    i = cap // PIECE
                    last = terms[i * PIECE : cap]
                    staged[j, :, i * width : end] = jnp.concatenate(
                        [last[:, : width // 2], last[:, width // 2 :]]
                    ).astype(staged.dtype)
                copies.append(
                    pltpu.make_async_copy(
                        staged.at[j, :, pl.ds(0, end)], outs[k].at[j], sems.at[j]
                    )
                )
                copies[-1].start()
            for c in copies:
                c.wait()


def up_terms(caps, way, select, low_mine, low_theirs, up_mine, up_theirs):
    chips, rank, width = up_mine.shape
    vmem = pl.BlockSpec(memory_space=pltpu.VMEM)
    shapes = [(chips, PIECE, cap * width // PIECE) for cap in caps]
    return pl.pallas_call(
        functools.partial(up_kernel, caps),
        in_specs=[pl.BlockSpec(memory_space=pltpu.SMEM)] + [vmem] * 5,
        out_specs=[pl.BlockSpec(memory_space=pl.ANY)] * len(caps),
        out_shape=[jax.ShapeDtypeStruct(shape, jnp.bfloat16) for shape in shapes],
        scratch_shapes=[
            pltpu.VMEM(shapes[-1], jnp.bfloat16),
            pltpu.SemaphoreType.DMA((chips,)),
        ],
        compiler_params=pltpu.CompilerParams(vmem_limit_bytes=16 * 2**20),
        cost_estimate=pl.CostEstimate(
            flops=4 * caps[-1] * rank * chips * width,
            bytes_accessed=2 * (2 * rank + caps[-1]) * chips * width,
            transcendentals=0,
        ),
        name="up_terms",
    )(way, select, low_mine, low_theirs, up_mine, up_theirs)


def add_kernel(base, received, pick, pick_right, out):
    rows, width = base.shape
    line, total = received.shape
    whole, part = total // width, total % width
    step = width // 2
    for half in range(2):
        columns = slice(half * step, (half + 1) * step)
        value = base[:, columns]
        for i in range(whole):
            piece = received[:, i * width + half * step : i * width + (half + 1) * step]
            value += jnp.dot(
                pick[:, i * line : (i + 1) * line], piece, preferred_element_type=jnp.float32
            )
        if part:
            choice = pick_right[...] if half else pick[:, whole * line : (whole + 1) * line]
            value += jnp.dot(
                choice, received[:, whole * width :], preferred_element_type=jnp.float32
            )
        out[:, columns] = value.astype(out.dtype)


def add_received(base, received, pick, pick_right):
    rows, width = base.shape
    vmem = pl.BlockSpec(memory_space=pltpu.VMEM)
    return pl.pallas_call(
        add_kernel,
        in_specs=[vmem] * 4,
        out_specs=vmem,
        out_shape=jax.ShapeDtypeStruct((rows, width), jnp.bfloat16),
        compiler_params=pltpu.CompilerParams(vmem_limit_bytes=24 * 2**20),
        cost_estimate=pl.CostEstimate(
            flops=4 * pick.size * width, bytes_accessed=8 * rows * width, transcendentals=0
        ),
        name="add_received",
    )(base, received.reshape(-1, received.shape[2]), pick, pick_right)


def chip_pool(
    normed_input_rows,
    gate_base_weight,
    adapter_down_factors,
    adapter_up_factors,
    request_adapter_id,
    row_request,
    adapter_storage_slot,
):
    npool, chips = 16, 8
    member = lax.axis_index("pool")

    def swap(value, bits):
        return lax.ppermute(value, "pool", [(i, i ^ bits) for i in range(npool)])

    far = swap(normed_input_rows, 8)
    near = swap(normed_input_rows, 4)
    side = swap(normed_input_rows, 2)
    far_near, far_diagonal = swap(far, 4), swap(far, 6)
    across = swap(jnp.concatenate([near, far]), 2)
    half = jnp.concatenate(
        [normed_input_rows, far, near, side, far_near, far_diagonal, across]
    )
    down, up = adapter_down_factors[0], adapter_up_factors[0]
    down_theirs = swap(down, 1)
    requests, rows = request_adapter_id.shape[0], row_request.shape[0]
    named = jnp.concatenate([row_request, request_adapter_id[:, 0], adapter_storage_slot])[None, :]
    select, way, up_mine, up_swapped = prepare(
        member, requests, named, up, chips, rows
    )
    up_theirs = swap(up_swapped, 1)

    half, up_theirs = lax.optimization_barrier((half, up_theirs))
    low_mine = low_values(half, down, down_theirs)
    low_theirs = swap(low_mine, 1)

    def exchange(terms):
        return lax.all_to_all(
            terms,
            "pool",
            split_axis=0,
            concat_axis=0,
            tiled=True,
            axis_index_groups=[[2 * i + c for i in range(chips)] for c in range(2)],
        )

    terms = up_terms(CHIP_CAPS, way, select, low_mine, low_theirs, up_mine, up_theirs)
    half, *terms = lax.optimization_barrier((half, *terms))

    def finish(k, half):
        received = exchange(terms[k])
        swapped, named_then = lax.optimization_barrier((swap(half, 1), named))
        pick, pick_right, order = picks(member, requests, named_then, chips, rows)
        x = jnp.concatenate([half, swapped])
        x = jnp.dot(order, x, preferred_element_type=jnp.float32).astype(jnp.bfloat16)
        base = jnp.dot(x, gate_base_weight, preferred_element_type=jnp.float32)
        base, received = lax.optimization_barrier((base, received))
        return add_received(base, received, pick, pick_right)

    ways = [functools.partial(finish, k) for k in range(len(CHIP_CAPS))]
    return lax.switch(way[0], ways, half)


def solution(mesh):
    in_specs = (
        P(("groups", "pool"), None),
        P(None, "pool"),
        P(("groups", "pool"), None, None),
        P(("groups", "pool"), None, None),
        P("groups", None),
        P("groups"),
        P("groups"),
    )
    out_specs = P("groups", "pool")

    def on_device(*blocks):
        width, share = blocks[1].shape[1], blocks[2].shape[0]
        chip_wise = mesh.shape["pool"] == 16 and width % 128 == 0 and share == 1
        return (chip_pool if chip_wise else any_pool)(*blocks)

    return jax.shard_map(
        on_device, mesh=mesh, in_specs=in_specs, out_specs=out_specs, check_vma=False
    )
```

```python
import functools

import jax
import jax.numpy as jnp
from jax import lax
from jax.experimental import pallas as pl
from jax.experimental.pallas import tpu as pltpu
from jax.sharding import PartitionSpec as P

ROW_CAP = 24
CHIP_CAPS = (24, 28, 32, 2 * ROW_CAP)
PIECE = 8


def slots_and_places(request_adapter_id, row_request, adapter_storage_slot, share):
    adapters = adapter_storage_slot.shape[0]
    requests = request_adapter_id.shape[0]
    request_slot = jnp.sum(
        jnp.where(
            request_adapter_id == jnp.arange(adapters, dtype=jnp.int32)[None, :],
            adapter_storage_slot[None, :],
            0,
        ),
        axis=1,
    )
    row_slot = jnp.sum(
        jnp.where(
            row_request[:, None] == jnp.arange(requests, dtype=jnp.int32)[None, :],
            request_slot[None, :],
            0,
        ),
        axis=1,
    )
    rows = row_slot.shape[0]
    holder = row_slot // share
    before = jnp.arange(rows)[None, :] < jnp.arange(rows)[:, None]
    place = jnp.sum((before & (holder[:, None] == holder[None, :])).astype(jnp.int32), axis=1)
    return row_slot, place


def add_terms(base, received, holder, place, cap):
    at = jnp.where(place < cap, holder * cap + place, -1)
    pick = (at[:, None] == jnp.arange(received.shape[0], dtype=jnp.int32)[None, :]).astype(
        jnp.bfloat16
    )
    return base + jnp.dot(pick, received, preferred_element_type=jnp.float32)


def any_pool(
    normed_input_rows,
    gate_base_weight,
    adapter_down_factors,
    adapter_up_factors,
    request_adapter_id,
    row_request,
    adapter_storage_slot,
):
    member = lax.axis_index("pool")
    share, rank = adapter_down_factors.shape[:2]
    row_slot, place = slots_and_places(
        request_adapter_id, row_request, adapter_storage_slot, share
    )
    owner = row_slot // share
    cap = share * ROW_CAP
    x = lax.all_gather(normed_input_rows, "pool", axis=0, tiled=True)
    select = (
        (place[None, :] == jnp.arange(cap, dtype=jnp.int32)[:, None])
        & (owner == member)[None, :]
    ).astype(jnp.bfloat16)
    low = jnp.dot(
        x,
        adapter_down_factors.reshape(share * rank, -1).T,
        preferred_element_type=jnp.float32,
    ).astype(jnp.bfloat16)
    which = row_slot - member * share
    mine = which[:, None] == jnp.arange(share * rank, dtype=jnp.int32)[None, :] // rank
    low = jnp.where(mine, low, 0)
    chosen = jnp.dot(select, low, preferred_element_type=jnp.float32).astype(jnp.bfloat16)
    terms = jnp.dot(
        chosen,
        adapter_up_factors.reshape(share * rank, -1),
        preferred_element_type=jnp.float32,
    ).astype(jnp.bfloat16)
    received = lax.all_to_all(terms, "pool", split_axis=1, concat_axis=0, tiled=True)
    base = jnp.dot(x, gate_base_weight, preferred_element_type=jnp.float32)
    base, received = lax.optimization_barrier((base, received))
    return add_terms(base, received, owner, place, cap).astype(jnp.bfloat16)


KEYS = (0, 8, 4, 2, 12, 14, 6, 10)


def start_columns(core, up, outs, sems):
    chips, _, width = outs[0].shape
    copies = []
    for which, out in enumerate(outs):
        for j in range(chips):
            at = pl.multiple_of((2 * j + (core ^ which)) * width, 128)
            copies.append(
                pltpu.make_async_copy(up.at[:, pl.ds(at, width)], out.at[j], sems.at[which, j])
            )
    for c in copies:
        c.start()
    return copies


def iota(shape, axis):
    return lax.broadcasted_iota(jnp.int32, shape, axis)


def where_sum(mask, values, axis):
    return jnp.sum(jnp.where(mask, values, 0), axis=axis, keepdims=True)


def one_hot(mask, out):
    return jnp.where(mask, 1.0, 0.0).astype(out.dtype)


def rows_and_places(me, rows, requests, named):
    row_request = named[:, :rows]
    request_id, slots = named[:, rows : rows + requests], named[:, rows + requests :]
    adapters = slots.shape[1]
    square = (requests, requests)
    request_down = where_sum(iota(square, 0) == iota(square, 1), request_id, 1)
    request_slot = where_sum(request_down == iota((requests, adapters), 1), slots, 1)
    slot = where_sum(row_request == iota((requests, rows), 0), request_slot, 0)
    down, along = iota((rows, rows), 0), iota((rows, rows), 1)
    slot_down = where_sum(down == along, slot, 1)
    same = slot_down // 2 == slot // 2
    place = where_sum(same & (down < along), jnp.ones((rows, rows), jnp.int32), 0)
    place_down = where_sum(same & (along < down), jnp.ones((rows, rows), jnp.int32), 1)

    lane = iota((1, rows), 1)
    side, lane = lane // (rows // 2), lane % (rows // 2)
    each = rows // (2 * len(KEYS))
    holder = jnp.zeros((1, rows), jnp.int32)
    for i, key in enumerate(KEYS):
        holder = jnp.where(lane // each == i, key, holder)
    actual = ((holder ^ side) ^ me) * each + lane % each
    return place, slot_down, place_down, actual, down


def rows_kernel(requests, member, named, up, select, way, here, there, sems):
    rows = select.shape[2]
    me = member[0]
    copies = start_columns(me & 1, up, (here, there), sems)
    place, slot_down, place_down, actual, down = rows_and_places(me, rows, requests, named)
    both = where_sum(down == actual, slot_down * rows + place_down, 0)
    slot_here, place_here = both // rows, both % rows
    placed = place_here == iota(select.shape[1:], 0)
    for which in range(2):
        select[which] = one_hot(placed & (slot_here == (me ^ which)), select)
    most = jnp.max(place)
    way[0] = sum((most >= cap).astype(jnp.int32) for cap in CHIP_CAPS[:-1])
    for c in copies:
        c.wait()


def picks_kernel(requests, member, named, pick, pick_right, order):
    rows = order.shape[0]
    _, slot_down, place_down, actual, down = rows_and_places(member[0], rows, requests, named)
    order[...] = one_hot(down == actual, order)
    line = pick_right.shape[1]
    at = place_down // PIECE * line + slot_down // 2 * PIECE + place_down % PIECE
    pick[...] = one_hot(at == iota(pick.shape, 1), pick)
    at = place_down % PIECE + PIECE // 2
    at = jnp.where((place_down // PIECE == 3) & (at < PIECE), slot_down // 2 * PIECE + at, -1)
    pick_right[...] = one_hot(at == iota(pick_right.shape, 1), pick_right)


def columns_shapes(up, chips):
    return [pltpu.VMEM((chips, up.shape[0], up.shape[1] // (2 * chips)), jnp.bfloat16)] * 2


def prepare(member, requests, named, up, chips, rows):
    smem, vmem = pl.BlockSpec(memory_space=pltpu.SMEM), pl.BlockSpec(memory_space=pltpu.VMEM)
    return pl.pallas_call(
        functools.partial(rows_kernel, requests),
        in_specs=[smem, vmem, pl.BlockSpec(memory_space=pl.ANY)],
        out_specs=[vmem, smem, vmem, vmem],
        out_shape=[
            pltpu.VMEM((2, CHIP_CAPS[-1], rows), jnp.bfloat16),
            jax.ShapeDtypeStruct((1,), jnp.int32),
            *columns_shapes(up, chips),
        ],
        scratch_shapes=[pltpu.SemaphoreType.DMA((2, chips))],
        compiler_params=pltpu.CompilerParams(vmem_limit_bytes=16 * 2**20),
        name="prepare",
    )(member.reshape(1), named, pltpu.with_memory_space_constraint(up, pltpu.HBM))


def picks(member, requests, named, chips, rows):
    vmem = pl.BlockSpec(memory_space=pltpu.VMEM)
    widths = (chips * CHIP_CAPS[-1], chips * PIECE, rows)
    return pl.pallas_call(
        functools.partial(picks_kernel, requests),
        in_specs=[pl.BlockSpec(memory_space=pltpu.SMEM), vmem],
        out_specs=[vmem] * 3,
        out_shape=[jax.ShapeDtypeStruct((rows, width), jnp.bfloat16) for width in widths],
        name="picks",
    )(member.reshape(1), named)


def low_kernel(half, down_mine, down_theirs, low):
    total = jnp.zeros(low.shape, jnp.float32)
    depth = half.shape[1] // 8
    for k in range(8):
        part = slice(k * depth, (k + 1) * depth)
        down = jnp.concatenate([down_mine[:, part], down_theirs[:, part]])
        total += lax.dot_general(
            half[:, part], down, (((1,), (1,)), ((), ())), preferred_element_type=jnp.float32
        )
    low[...] = total.astype(low.dtype)


def low_values(half, down_mine, down_theirs):
    rank = down_mine.shape[0]
    vmem = pl.BlockSpec(memory_space=pltpu.VMEM)
    return pl.pallas_call(
        low_kernel,
        in_specs=[vmem] * 3,
        out_specs=vmem,
        out_shape=pltpu.VMEM((half.shape[0], 2 * rank), jnp.bfloat16),
        compiler_params=pltpu.CompilerParams(vmem_limit_bytes=16 * 2**20),
        cost_estimate=pl.CostEstimate(
            flops=4 * half.size * rank, bytes_accessed=2 * half.size, transcendentals=0
        ),
        name="low_values",
    )(half, down_mine, down_theirs)


def up_kernel(caps, way, select, low_mine, low_theirs, up_mine, up_theirs, *refs):
    outs, staged, sems = refs[: len(caps)], refs[-2], refs[-1]
    chips, rank, width = up_mine.shape
    taken = [way[0] == k for k in range(len(caps))]

    chosen = []
    for which in range(2):
        here = slice(which * rank, (which + 1) * rank)
        there = slice((1 - which) * rank, (2 - which) * rank)
        low = jnp.concatenate([low_mine[:, here], low_theirs[:, there]])
        chosen.append(jnp.dot(select[which], low, preferred_element_type=jnp.float32))
    low = jnp.concatenate(chosen, axis=1).astype(jnp.bfloat16)
    for k, cap in enumerate(caps):

        @pl.when(taken[k])
        def _():
            kept = low[: max(cap, caps[-2])]
            copies = []
            for j in range(chips):
                terms = jnp.dot(
                    kept,
                    jnp.concatenate([up_mine[j], up_theirs[j]]),
                    preferred_element_type=jnp.float32,
                )
                for i in range(cap // PIECE):
                    staged[j, :, i * width : (i + 1) * width] = terms[
                        i * PIECE : (i + 1) * PIECE
                    ].astype(staged.dtype)
                end = cap * width // PIECE
                if cap % PIECE:
                    i = cap // PIECE
                    last = terms[i * PIECE : cap]
                    staged[j, :, i * width : end] = jnp.concatenate(
                        [last[:, : width // 2], last[:, width // 2 :]]
                    ).astype(staged.dtype)
                copies.append(
                    pltpu.make_async_copy(
                        staged.at[j, :, pl.ds(0, end)], outs[k].at[j], sems.at[j]
                    )
                )
                copies[-1].start()
            for c in copies:
                c.wait()


def up_terms(caps, way, select, low_mine, low_theirs, up_mine, up_theirs):
    chips, rank, width = up_mine.shape
    vmem = pl.BlockSpec(memory_space=pltpu.VMEM)
    shapes = [(chips, PIECE, cap * width // PIECE) for cap in caps]
    return pl.pallas_call(
        functools.partial(up_kernel, caps),
        in_specs=[pl.BlockSpec(memory_space=pltpu.SMEM)] + [vmem] * 5,
        out_specs=[pl.BlockSpec(memory_space=pl.ANY)] * len(caps),
        out_shape=[jax.ShapeDtypeStruct(shape, jnp.bfloat16) for shape in shapes],
        scratch_shapes=[
            pltpu.VMEM(shapes[-1], jnp.bfloat16),
            pltpu.SemaphoreType.DMA((chips,)),
        ],
        compiler_params=pltpu.CompilerParams(vmem_limit_bytes=16 * 2**20),
        cost_estimate=pl.CostEstimate(
            flops=4 * caps[-1] * rank * chips * width,
            bytes_accessed=2 * (2 * rank + caps[-1]) * chips * width,
            transcendentals=0,
        ),
        name="up_terms",
    )(way, select, low_mine, low_theirs, up_mine, up_theirs)


def add_kernel(base, received, pick, pick_right, out):
    rows, width = base.shape
    line, total = received.shape
    whole, part = total // width, total % width
    step = width // 2
    for half in range(2):
        columns = slice(half * step, (half + 1) * step)
        value = base[:, columns]
        for i in range(whole):
            piece = received[:, i * width + half * step : i * width + (half + 1) * step]
            value += jnp.dot(
                pick[:, i * line : (i + 1) * line], piece, preferred_element_type=jnp.float32
            )
        if part:
            choice = pick_right[...] if half else pick[:, whole * line : (whole + 1) * line]
            value += jnp.dot(
                choice, received[:, whole * width :], preferred_element_type=jnp.float32
            )
        out[:, columns] = value.astype(out.dtype)


def add_received(base, received, pick, pick_right):
    rows, width = base.shape
    vmem = pl.BlockSpec(memory_space=pltpu.VMEM)
    return pl.pallas_call(
        add_kernel,
        in_specs=[vmem] * 4,
        out_specs=vmem,
        out_shape=jax.ShapeDtypeStruct((rows, width), jnp.bfloat16),
        compiler_params=pltpu.CompilerParams(vmem_limit_bytes=24 * 2**20),
        cost_estimate=pl.CostEstimate(
            flops=4 * pick.size * width, bytes_accessed=8 * rows * width, transcendentals=0
        ),
        name="add_received",
    )(base, received.reshape(-1, received.shape[2]), pick, pick_right)


def chip_pool(
    normed_input_rows,
    gate_base_weight,
    adapter_down_factors,
    adapter_up_factors,
    request_adapter_id,
    row_request,
    adapter_storage_slot,
):
    npool, chips = 16, 8
    member = lax.axis_index("pool")

    def swap(value, bits):
        return lax.ppermute(value, "pool", [(i, i ^ bits) for i in range(npool)])

    far = swap(normed_input_rows, 8)
    near = swap(normed_input_rows, 4)
    side = swap(normed_input_rows, 2)
    near, side = lax.optimization_barrier((near, side))
    side_across, far_near = swap(side, 12), swap(far, 4)
    across = swap(jnp.concatenate([near, far]), 2)
    half = jnp.concatenate(
        [normed_input_rows, far, near, side, far_near, side_across, across]
    )
    down, up = adapter_down_factors[0], adapter_up_factors[0]
    down_theirs = swap(down, 1)
    requests, rows = request_adapter_id.shape[0], row_request.shape[0]
    named = jnp.concatenate([row_request, request_adapter_id[:, 0], adapter_storage_slot])[None, :]
    select, way, up_mine, up_swapped = prepare(
        member, requests, named, up, chips, rows
    )
    up_theirs = swap(up_swapped, 1)

    half, up_theirs = lax.optimization_barrier((half, up_theirs))
    low_mine = low_values(half, down, down_theirs)
    low_theirs = swap(low_mine, 1)

    def exchange(terms):
        return lax.all_to_all(
            terms,
            "pool",
            split_axis=0,
            concat_axis=0,
            tiled=True,
            axis_index_groups=[[2 * i + c for i in range(chips)] for c in range(2)],
        )

    terms = up_terms(CHIP_CAPS, way, select, low_mine, low_theirs, up_mine, up_theirs)
    half, *terms = lax.optimization_barrier((half, *terms))

    def finish(k, half):
        received = exchange(terms[k])
        swapped, named_then = lax.optimization_barrier((swap(half, 1), named))
        pick, pick_right, order = picks(member, requests, named_then, chips, rows)
        x = jnp.concatenate([half, swapped])
        x = jnp.dot(order, x, preferred_element_type=jnp.float32).astype(jnp.bfloat16)
        base = jnp.dot(x, gate_base_weight, preferred_element_type=jnp.float32)
        base, received = lax.optimization_barrier((base, received))
        return add_received(base, received, pick, pick_right)

    ways = [functools.partial(finish, k) for k in range(len(CHIP_CAPS))]
    return lax.switch(way[0], ways, half)


def solution(mesh):
    in_specs = (
        P(("groups", "pool"), None),
        P(None, "pool"),
        P(("groups", "pool"), None, None),
        P(("groups", "pool"), None, None),
        P("groups", None),
        P("groups"),
        P("groups"),
    )
    out_specs = P("groups", "pool")

    def on_device(*blocks):
        width, share = blocks[1].shape[1], blocks[2].shape[0]
        chip_wise = mesh.shape["pool"] == 16 and width % 128 == 0 and share == 1
        return (chip_pool if chip_wise else any_pool)(*blocks)

    return jax.shard_map(
        on_device, mesh=mesh, in_specs=in_specs, out_specs=out_specs, check_vma=False
    )
```

```python
import functools

import jax
import jax.numpy as jnp
from jax import lax
from jax.experimental import pallas as pl
from jax.experimental.pallas import tpu as pltpu
from jax.sharding import PartitionSpec as P

ROW_CAP = 24
CHIP_CAPS = (24, 28, 32, 2 * ROW_CAP)
PIECE = 8


def slots_and_places(request_adapter_id, row_request, adapter_storage_slot, share):
    adapters = adapter_storage_slot.shape[0]
    requests = request_adapter_id.shape[0]
    request_slot = jnp.sum(
        jnp.where(
            request_adapter_id == jnp.arange(adapters, dtype=jnp.int32)[None, :],
            adapter_storage_slot[None, :],
            0,
        ),
        axis=1,
    )
    row_slot = jnp.sum(
        jnp.where(
            row_request[:, None] == jnp.arange(requests, dtype=jnp.int32)[None, :],
            request_slot[None, :],
            0,
        ),
        axis=1,
    )
    rows = row_slot.shape[0]
    holder = row_slot // share
    before = jnp.arange(rows)[None, :] < jnp.arange(rows)[:, None]
    place = jnp.sum((before & (holder[:, None] == holder[None, :])).astype(jnp.int32), axis=1)
    return row_slot, place


def add_terms(base, received, holder, place, cap):
    at = jnp.where(place < cap, holder * cap + place, -1)
    pick = (at[:, None] == jnp.arange(received.shape[0], dtype=jnp.int32)[None, :]).astype(
        jnp.bfloat16
    )
    return base + jnp.dot(pick, received, preferred_element_type=jnp.float32)


def any_pool(
    normed_input_rows,
    gate_base_weight,
    adapter_down_factors,
    adapter_up_factors,
    request_adapter_id,
    row_request,
    adapter_storage_slot,
):
    member = lax.axis_index("pool")
    share, rank = adapter_down_factors.shape[:2]
    row_slot, place = slots_and_places(
        request_adapter_id, row_request, adapter_storage_slot, share
    )
    owner = row_slot // share
    cap = share * ROW_CAP
    x = lax.all_gather(normed_input_rows, "pool", axis=0, tiled=True)
    select = (
        (place[None, :] == jnp.arange(cap, dtype=jnp.int32)[:, None])
        & (owner == member)[None, :]
    ).astype(jnp.bfloat16)
    low = jnp.dot(
        x,
        adapter_down_factors.reshape(share * rank, -1).T,
        preferred_element_type=jnp.float32,
    ).astype(jnp.bfloat16)
    which = row_slot - member * share
    mine = which[:, None] == jnp.arange(share * rank, dtype=jnp.int32)[None, :] // rank
    low = jnp.where(mine, low, 0)
    chosen = jnp.dot(select, low, preferred_element_type=jnp.float32).astype(jnp.bfloat16)
    terms = jnp.dot(
        chosen,
        adapter_up_factors.reshape(share * rank, -1),
        preferred_element_type=jnp.float32,
    ).astype(jnp.bfloat16)
    received = lax.all_to_all(terms, "pool", split_axis=1, concat_axis=0, tiled=True)
    base = jnp.dot(x, gate_base_weight, preferred_element_type=jnp.float32)
    base, received = lax.optimization_barrier((base, received))
    return add_terms(base, received, owner, place, cap).astype(jnp.bfloat16)


KEYS = (0, 8, 4, 2, 14, 6, 10, 12)


def start_columns(core, up, outs, sems):
    chips, _, width = outs[0].shape
    copies = []
    for which, out in enumerate(outs):
        for j in range(chips):
            at = pl.multiple_of((2 * j + (core ^ which)) * width, 128)
            copies.append(
                pltpu.make_async_copy(up.at[:, pl.ds(at, width)], out.at[j], sems.at[which, j])
            )
    for c in copies:
        c.start()
    return copies


def iota(shape, axis):
    return lax.broadcasted_iota(jnp.int32, shape, axis)


def where_sum(mask, values, axis):
    return jnp.sum(jnp.where(mask, values, 0), axis=axis, keepdims=True)


def one_hot(mask, out):
    return jnp.where(mask, 1.0, 0.0).astype(out.dtype)


def rows_and_places(me, rows, requests, named):
    row_request = named[:, :rows]
    request_id, slots = named[:, rows : rows + requests], named[:, rows + requests :]
    adapters = slots.shape[1]
    square = (requests, requests)
    request_down = where_sum(iota(square, 0) == iota(square, 1), request_id, 1)
    request_slot = where_sum(request_down == iota((requests, adapters), 1), slots, 1)
    slot = where_sum(row_request == iota((requests, rows), 0), request_slot, 0)
    down, along = iota((rows, rows), 0), iota((rows, rows), 1)
    slot_down = where_sum(down == along, slot, 1)
    same = slot_down // 2 == slot // 2
    place = where_sum(same & (down < along), jnp.ones((rows, rows), jnp.int32), 0)
    place_down = where_sum(same & (along < down), jnp.ones((rows, rows), jnp.int32), 1)

    lane = iota((1, rows), 1)
    side, lane = lane // (rows // 2), lane % (rows // 2)
    each = rows // (2 * len(KEYS))
    holder = jnp.zeros((1, rows), jnp.int32)
    for i, key in enumerate(KEYS):
        holder = jnp.where(lane // each == i, key, holder)
    actual = ((holder ^ side) ^ me) * each + lane % each
    return place, slot_down, place_down, actual, down


def rows_kernel(requests, member, named, up, select, way, here, there, sems):
    rows = select.shape[2]
    me = member[0]
    copies = start_columns(me & 1, up, (here, there), sems)
    place, slot_down, place_down, actual, down = rows_and_places(me, rows, requests, named)
    both = where_sum(down == actual, slot_down * rows + place_down, 0)
    slot_here, place_here = both // rows, both % rows
    placed = place_here == iota(select.shape[1:], 0)
    for which in range(2):
        select[which] = one_hot(placed & (slot_here == (me ^ which)), select)
    most = jnp.max(place)
    way[0] = sum((most >= cap).astype(jnp.int32) for cap in CHIP_CAPS[:-1])
    for c in copies:
        c.wait()


def picks_kernel(requests, member, named, pick, pick_right, order):
    rows = order.shape[0]
    _, slot_down, place_down, actual, down = rows_and_places(member[0], rows, requests, named)
    order[...] = one_hot(down == actual, order)
    line = pick_right.shape[1]
    at = place_down // PIECE * line + slot_down // 2 * PIECE + place_down % PIECE
    pick[...] = one_hot(at == iota(pick.shape, 1), pick)
    at = place_down % PIECE + PIECE // 2
    at = jnp.where((place_down // PIECE == 3) & (at < PIECE), slot_down // 2 * PIECE + at, -1)
    pick_right[...] = one_hot(at == iota(pick_right.shape, 1), pick_right)


def columns_shapes(up, chips):
    return [pltpu.VMEM((chips, up.shape[0], up.shape[1] // (2 * chips)), jnp.bfloat16)] * 2


def prepare(member, requests, named, up, chips, rows):
    smem, vmem = pl.BlockSpec(memory_space=pltpu.SMEM), pl.BlockSpec(memory_space=pltpu.VMEM)
    return pl.pallas_call(
        functools.partial(rows_kernel, requests),
        in_specs=[smem, vmem, pl.BlockSpec(memory_space=pl.ANY)],
        out_specs=[vmem, smem, vmem, vmem],
        out_shape=[
            pltpu.VMEM((2, CHIP_CAPS[-1], rows), jnp.bfloat16),
            jax.ShapeDtypeStruct((1,), jnp.int32),
            *columns_shapes(up, chips),
        ],
        scratch_shapes=[pltpu.SemaphoreType.DMA((2, chips))],
        compiler_params=pltpu.CompilerParams(vmem_limit_bytes=16 * 2**20),
        name="prepare",
    )(member.reshape(1), named, pltpu.with_memory_space_constraint(up, pltpu.HBM))


def picks(member, requests, named, chips, rows):
    vmem = pl.BlockSpec(memory_space=pltpu.VMEM)
    widths = (chips * CHIP_CAPS[-1], chips * PIECE, rows)
    return pl.pallas_call(
        functools.partial(picks_kernel, requests),
        in_specs=[pl.BlockSpec(memory_space=pltpu.SMEM), vmem],
        out_specs=[vmem] * 3,
        out_shape=[jax.ShapeDtypeStruct((rows, width), jnp.bfloat16) for width in widths],
        name="picks",
    )(member.reshape(1), named)


def low_kernel(half, down_mine, down_theirs, low):
    total = jnp.zeros(low.shape, jnp.float32)
    depth = half.shape[1] // 8
    for k in range(8):
        part = slice(k * depth, (k + 1) * depth)
        down = jnp.concatenate([down_mine[:, part], down_theirs[:, part]])
        total += lax.dot_general(
            half[:, part], down, (((1,), (1,)), ((), ())), preferred_element_type=jnp.float32
        )
    low[...] = total.astype(low.dtype)


def low_values(half, down_mine, down_theirs):
    rank = down_mine.shape[0]
    vmem = pl.BlockSpec(memory_space=pltpu.VMEM)
    return pl.pallas_call(
        low_kernel,
        in_specs=[vmem] * 3,
        out_specs=vmem,
        out_shape=pltpu.VMEM((half.shape[0], 2 * rank), jnp.bfloat16),
        compiler_params=pltpu.CompilerParams(vmem_limit_bytes=16 * 2**20),
        cost_estimate=pl.CostEstimate(
            flops=4 * half.size * rank, bytes_accessed=2 * half.size, transcendentals=0
        ),
        name="low_values",
    )(half, down_mine, down_theirs)


def up_kernel(caps, way, select, low_mine, low_theirs, up_mine, up_theirs, *refs):
    outs, staged, sems = refs[: len(caps)], refs[-2], refs[-1]
    chips, rank, width = up_mine.shape
    taken = [way[0] == k for k in range(len(caps))]

    chosen = []
    for which in range(2):
        here = slice(which * rank, (which + 1) * rank)
        there = slice((1 - which) * rank, (2 - which) * rank)
        low = jnp.concatenate([low_mine[:, here], low_theirs[:, there]])
        chosen.append(jnp.dot(select[which], low, preferred_element_type=jnp.float32))
    low = jnp.concatenate(chosen, axis=1).astype(jnp.bfloat16)
    for k, cap in enumerate(caps):

        @pl.when(taken[k])
        def _():
            kept = low[: max(cap, caps[-2])]
            end = cap * width // PIECE
            part = chips // 2
            copies = []
            for j in range(chips):
                terms = jnp.dot(
                    kept,
                    jnp.concatenate([up_mine[j], up_theirs[j]]),
                    preferred_element_type=jnp.float32,
                )
                for i in range(cap // PIECE):
                    staged[j, :, i * width : (i + 1) * width] = terms[
                        i * PIECE : (i + 1) * PIECE
                    ].astype(staged.dtype)
                if cap % PIECE:
                    i = cap // PIECE
                    last = terms[i * PIECE : cap]
                    staged[j, :, i * width : end] = jnp.concatenate(
                        [last[:, : width // 2], last[:, width // 2 :]]
                    ).astype(staged.dtype)
                if j % part == part - 1:
                    some = pl.ds(j + 1 - part, part)
                    copies.append(
                        pltpu.make_async_copy(
                            staged.at[some, :, pl.ds(0, end)],
                            outs[k].at[some],
                            sems.at[j // part],
                        )
                    )
                    copies[-1].start()
            for c in copies:
                c.wait()


def up_terms(caps, way, select, low_mine, low_theirs, up_mine, up_theirs):
    chips, rank, width = up_mine.shape
    vmem = pl.BlockSpec(memory_space=pltpu.VMEM)
    shapes = [(chips, PIECE, cap * width // PIECE) for cap in caps]
    return pl.pallas_call(
        functools.partial(up_kernel, caps),
        in_specs=[pl.BlockSpec(memory_space=pltpu.SMEM)] + [vmem] * 5,
        out_specs=[pl.BlockSpec(memory_space=pl.ANY)] * len(caps),
        out_shape=[jax.ShapeDtypeStruct(shape, jnp.bfloat16) for shape in shapes],
        scratch_shapes=[
            pltpu.VMEM(shapes[-1], jnp.bfloat16),
            pltpu.SemaphoreType.DMA((2,)),
        ],
        compiler_params=pltpu.CompilerParams(vmem_limit_bytes=16 * 2**20),
        cost_estimate=pl.CostEstimate(
            flops=4 * caps[-1] * rank * chips * width,
            bytes_accessed=2 * (2 * rank + caps[-1]) * chips * width,
            transcendentals=0,
        ),
        name="up_terms",
    )(way, select, low_mine, low_theirs, up_mine, up_theirs)


def add_kernel(base, received, pick, pick_right, out):
    rows, width = base.shape
    line, total = received.shape
    whole, part = total // width, total % width
    step = width // 2
    for half in range(2):
        columns = slice(half * step, (half + 1) * step)
        value = base[:, columns]
        for i in range(whole):
            piece = received[:, i * width + half * step : i * width + (half + 1) * step]
            value += jnp.dot(
                pick[:, i * line : (i + 1) * line], piece, preferred_element_type=jnp.float32
            )
        if part:
            choice = pick_right[...] if half else pick[:, whole * line : (whole + 1) * line]
            value += jnp.dot(
                choice, received[:, whole * width :], preferred_element_type=jnp.float32
            )
        out[:, columns] = value.astype(out.dtype)


def add_received(base, received, pick, pick_right):
    rows, width = base.shape
    vmem = pl.BlockSpec(memory_space=pltpu.VMEM)
    return pl.pallas_call(
        add_kernel,
        in_specs=[vmem] * 4,
        out_specs=vmem,
        out_shape=jax.ShapeDtypeStruct((rows, width), jnp.bfloat16),
        compiler_params=pltpu.CompilerParams(vmem_limit_bytes=24 * 2**20),
        cost_estimate=pl.CostEstimate(
            flops=4 * pick.size * width, bytes_accessed=8 * rows * width, transcendentals=0
        ),
        name="add_received",
    )(base, received.reshape(-1, received.shape[2]), pick, pick_right)


def chip_pool(
    normed_input_rows,
    gate_base_weight,
    adapter_down_factors,
    adapter_up_factors,
    request_adapter_id,
    row_request,
    adapter_storage_slot,
):
    npool, chips = 16, 8
    member = lax.axis_index("pool")

    def swap(value, bits):
        return lax.ppermute(value, "pool", [(i, i ^ bits) for i in range(npool)])

    far = swap(normed_input_rows, 8)
    near = swap(normed_input_rows, 4)
    side = swap(normed_input_rows, 2)
    near, side = lax.optimization_barrier((near, side))
    side_across, far_near = swap(side, 12), swap(far, 4)
    across = swap(jnp.concatenate([near, far]), 2)
    half = jnp.concatenate(
        [normed_input_rows, far, near, side, side_across, across, far_near]
    )
    down, up = adapter_down_factors[0], adapter_up_factors[0]
    down_theirs = swap(down, 1)
    requests, rows = request_adapter_id.shape[0], row_request.shape[0]
    named = jnp.concatenate([row_request, request_adapter_id[:, 0], adapter_storage_slot])[None, :]
    select, way, up_mine, up_swapped = prepare(
        member, requests, named, up, chips, rows
    )
    up_theirs = swap(up_swapped, 1)

    half, up_theirs = lax.optimization_barrier((half, up_theirs))
    low_mine = low_values(half, down, down_theirs)
    low_theirs = swap(low_mine, 1)

    def exchange(terms):
        return lax.all_to_all(
            terms,
            "pool",
            split_axis=0,
            concat_axis=0,
            tiled=True,
            axis_index_groups=[[2 * i + c for i in range(chips)] for c in range(2)],
        )

    terms = up_terms(CHIP_CAPS, way, select, low_mine, low_theirs, up_mine, up_theirs)
    half, *terms = lax.optimization_barrier((half, *terms))

    def finish(k, half):
        received = exchange(terms[k])
        swapped, named_then = lax.optimization_barrier((swap(half, 1), named))
        pick, pick_right, order = picks(member, requests, named_then, chips, rows)
        x = jnp.concatenate([half, swapped])
        x = jnp.dot(order, x, preferred_element_type=jnp.float32).astype(jnp.bfloat16)
        base = jnp.dot(x, gate_base_weight, preferred_element_type=jnp.float32)
        base, received = lax.optimization_barrier((base, received))
        return add_received(base, received, pick, pick_right)

    ways = [functools.partial(finish, k) for k in range(len(CHIP_CAPS))]
    return lax.switch(way[0], ways, half)


def solution(mesh):
    in_specs = (
        P(("groups", "pool"), None),
        P(None, "pool"),
        P(("groups", "pool"), None, None),
        P(("groups", "pool"), None, None),
        P("groups", None),
        P("groups"),
        P("groups"),
    )
    out_specs = P("groups", "pool")

    def on_device(*blocks):
        width, share = blocks[1].shape[1], blocks[2].shape[0]
        chip_wise = mesh.shape["pool"] == 16 and width % 128 == 0 and share == 1
        return (chip_pool if chip_wise else any_pool)(*blocks)

    return jax.shard_map(
        on_device, mesh=mesh, in_specs=in_specs, out_specs=out_specs, check_vma=False
    )
```

```python
import functools

import jax
import jax.numpy as jnp
from jax import lax
from jax.experimental import pallas as pl
from jax.experimental.pallas import tpu as pltpu
from jax.sharding import PartitionSpec as P

ROW_CAP = 24
CHIP_CAPS = (24, 28, 32, 40, 2 * ROW_CAP)
PIECE = 8


def slots_and_places(request_adapter_id, row_request, adapter_storage_slot, share):
    adapters = adapter_storage_slot.shape[0]
    requests = request_adapter_id.shape[0]
    request_slot = jnp.sum(
        jnp.where(
            request_adapter_id == jnp.arange(adapters, dtype=jnp.int32)[None, :],
            adapter_storage_slot[None, :],
            0,
        ),
        axis=1,
    )
    row_slot = jnp.sum(
        jnp.where(
            row_request[:, None] == jnp.arange(requests, dtype=jnp.int32)[None, :],
            request_slot[None, :],
            0,
        ),
        axis=1,
    )
    rows = row_slot.shape[0]
    holder = row_slot // share
    before = jnp.arange(rows)[None, :] < jnp.arange(rows)[:, None]
    place = jnp.sum((before & (holder[:, None] == holder[None, :])).astype(jnp.int32), axis=1)
    return row_slot, place


def add_terms(base, received, holder, place, cap):
    at = jnp.where(place < cap, holder * cap + place, -1)
    pick = (at[:, None] == jnp.arange(received.shape[0], dtype=jnp.int32)[None, :]).astype(
        jnp.bfloat16
    )
    return base + jnp.dot(pick, received, preferred_element_type=jnp.float32)


def any_pool(
    normed_input_rows,
    gate_base_weight,
    adapter_down_factors,
    adapter_up_factors,
    request_adapter_id,
    row_request,
    adapter_storage_slot,
):
    member = lax.axis_index("pool")
    share, rank = adapter_down_factors.shape[:2]
    row_slot, place = slots_and_places(
        request_adapter_id, row_request, adapter_storage_slot, share
    )
    owner = row_slot // share
    cap = share * ROW_CAP
    x = lax.all_gather(normed_input_rows, "pool", axis=0, tiled=True)
    select = (
        (place[None, :] == jnp.arange(cap, dtype=jnp.int32)[:, None])
        & (owner == member)[None, :]
    ).astype(jnp.bfloat16)
    low = jnp.dot(
        x,
        adapter_down_factors.reshape(share * rank, -1).T,
        preferred_element_type=jnp.float32,
    ).astype(jnp.bfloat16)
    which = row_slot - member * share
    mine = which[:, None] == jnp.arange(share * rank, dtype=jnp.int32)[None, :] // rank
    low = jnp.where(mine, low, 0)
    chosen = jnp.dot(select, low, preferred_element_type=jnp.float32).astype(jnp.bfloat16)
    terms = jnp.dot(
        chosen,
        adapter_up_factors.reshape(share * rank, -1),
        preferred_element_type=jnp.float32,
    ).astype(jnp.bfloat16)
    received = lax.all_to_all(terms, "pool", split_axis=1, concat_axis=0, tiled=True)
    base = jnp.dot(x, gate_base_weight, preferred_element_type=jnp.float32)
    base, received = lax.optimization_barrier((base, received))
    return add_terms(base, received, owner, place, cap).astype(jnp.bfloat16)


KEYS = (0, 8, 4, 2, 14, 6, 10, 12)


def start_columns(core, up, outs, sems):
    chips, _, width = outs[0].shape
    copies = []
    for which, out in enumerate(outs):
        for j in range(chips):
            at = pl.multiple_of((2 * j + (core ^ which)) * width, 128)
            copies.append(
                pltpu.make_async_copy(up.at[:, pl.ds(at, width)], out.at[j], sems.at[which, j])
            )
    for c in copies:
        c.start()
    return copies


def iota(shape, axis):
    return lax.broadcasted_iota(jnp.int32, shape, axis)


def where_sum(mask, values, axis):
    return jnp.sum(jnp.where(mask, values, 0), axis=axis, keepdims=True)


def one_hot(mask, out):
    return jnp.where(mask, 1.0, 0.0).astype(out.dtype)


def rows_and_places(me, rows, requests, named):
    row_request = named[:, :rows]
    request_id, slots = named[:, rows : rows + requests], named[:, rows + requests :]
    adapters = slots.shape[1]
    square = (requests, requests)
    request_down = where_sum(iota(square, 0) == iota(square, 1), request_id, 1)
    request_slot = where_sum(request_down == iota((requests, adapters), 1), slots, 1)
    slot = where_sum(row_request == iota((requests, rows), 0), request_slot, 0)
    down, along = iota((rows, rows), 0), iota((rows, rows), 1)
    slot_down = where_sum(down == along, slot, 1)
    same = slot_down // 2 == slot // 2
    place = where_sum(same & (down < along), jnp.ones((rows, rows), jnp.int32), 0)
    place_down = where_sum(same & (along < down), jnp.ones((rows, rows), jnp.int32), 1)

    lane = iota((1, rows), 1)
    side, lane = lane // (rows // 2), lane % (rows // 2)
    each = rows // (2 * len(KEYS))
    holder = jnp.zeros((1, rows), jnp.int32)
    for i, key in enumerate(KEYS):
        holder = jnp.where(lane // each == i, key, holder)
    actual = ((holder ^ side) ^ me) * each + lane % each
    return place, slot_down, place_down, actual, down


def rows_kernel(requests, member, named, up, select, way, here, there, sems):
    rows = select.shape[2]
    me = member[0]
    copies = start_columns(me & 1, up, (here, there), sems)
    place, slot_down, place_down, actual, down = rows_and_places(me, rows, requests, named)
    both = where_sum(down == actual, slot_down * rows + place_down, 0)
    slot_here, place_here = both // rows, both % rows
    placed = place_here == iota(select.shape[1:], 0)
    for which in range(2):
        select[which] = one_hot(placed & (slot_here == (me ^ which)), select)
    most = jnp.max(place)
    way[0] = sum((most >= cap).astype(jnp.int32) for cap in CHIP_CAPS[:-1])
    for c in copies:
        c.wait()


def picks_kernel(requests, member, named, pick, pick_right, order):
    rows = order.shape[0]
    _, slot_down, place_down, actual, down = rows_and_places(member[0], rows, requests, named)
    order[...] = one_hot(down == actual, order)
    line = pick_right.shape[1]
    at = place_down // PIECE * line + slot_down // 2 * PIECE + place_down % PIECE
    pick[...] = one_hot(at == iota(pick.shape, 1), pick)
    at = place_down % PIECE + PIECE // 2
    at = jnp.where((place_down // PIECE == 3) & (at < PIECE), slot_down // 2 * PIECE + at, -1)
    pick_right[...] = one_hot(at == iota(pick_right.shape, 1), pick_right)


def columns_shapes(up, chips):
    return [pltpu.VMEM((chips, up.shape[0], up.shape[1] // (2 * chips)), jnp.bfloat16)] * 2


def prepare(member, requests, named, up, chips, rows):
    smem, vmem = pl.BlockSpec(memory_space=pltpu.SMEM), pl.BlockSpec(memory_space=pltpu.VMEM)
    return pl.pallas_call(
        functools.partial(rows_kernel, requests),
        in_specs=[smem, vmem, pl.BlockSpec(memory_space=pl.ANY)],
        out_specs=[vmem, smem, vmem, vmem],
        out_shape=[
            pltpu.VMEM((2, CHIP_CAPS[-1], rows), jnp.bfloat16),
            jax.ShapeDtypeStruct((1,), jnp.int32),
            *columns_shapes(up, chips),
        ],
        scratch_shapes=[pltpu.SemaphoreType.DMA((2, chips))],
        compiler_params=pltpu.CompilerParams(vmem_limit_bytes=16 * 2**20),
        name="prepare",
    )(member.reshape(1), named, pltpu.with_memory_space_constraint(up, pltpu.HBM))


def picks(member, requests, named, chips, rows):
    vmem = pl.BlockSpec(memory_space=pltpu.VMEM)
    widths = (chips * CHIP_CAPS[-1], chips * PIECE, rows)
    return pl.pallas_call(
        functools.partial(picks_kernel, requests),
        in_specs=[pl.BlockSpec(memory_space=pltpu.SMEM), vmem],
        out_specs=[vmem] * 3,
        out_shape=[jax.ShapeDtypeStruct((rows, width), jnp.bfloat16) for width in widths],
        name="picks",
    )(member.reshape(1), named)


def low_kernel(half, down_mine, down_theirs, low):
    total = jnp.zeros(low.shape, jnp.float32)
    depth = half.shape[1] // 8
    for k in range(8):
        part = slice(k * depth, (k + 1) * depth)
        down = jnp.concatenate([down_mine[:, part], down_theirs[:, part]])
        total += lax.dot_general(
            half[:, part], down, (((1,), (1,)), ((), ())), preferred_element_type=jnp.float32
        )
    low[...] = total.astype(low.dtype)


def low_values(half, down_mine, down_theirs):
    rank = down_mine.shape[0]
    vmem = pl.BlockSpec(memory_space=pltpu.VMEM)
    return pl.pallas_call(
        low_kernel,
        in_specs=[vmem] * 3,
        out_specs=vmem,
        out_shape=pltpu.VMEM((half.shape[0], 2 * rank), jnp.bfloat16),
        compiler_params=pltpu.CompilerParams(vmem_limit_bytes=16 * 2**20),
        cost_estimate=pl.CostEstimate(
            flops=4 * half.size * rank, bytes_accessed=2 * half.size, transcendentals=0
        ),
        name="low_values",
    )(half, down_mine, down_theirs)


def up_kernel(caps, way, select, low_mine, low_theirs, up_mine, up_theirs, *refs):
    outs, staged, sems = refs[: len(caps)], refs[-2], refs[-1]
    chips, rank, width = up_mine.shape
    taken = [way[0] == k for k in range(len(caps))]

    chosen = []
    for which in range(2):
        here = slice(which * rank, (which + 1) * rank)
        there = slice((1 - which) * rank, (2 - which) * rank)
        low = jnp.concatenate([low_mine[:, here], low_theirs[:, there]])
        chosen.append(jnp.dot(select[which], low, preferred_element_type=jnp.float32))
    low = jnp.concatenate(chosen, axis=1).astype(jnp.bfloat16)
    for k, cap in enumerate(caps):

        @pl.when(taken[k])
        def _():
            kept = low[: -(-cap // 16) * 16]
            end = cap * width // PIECE
            part = chips // 2
            copies = []
            for j in range(chips):
                terms = jnp.dot(
                    kept,
                    jnp.concatenate([up_mine[j], up_theirs[j]]),
                    preferred_element_type=jnp.float32,
                )
                for i in range(cap // PIECE):
                    staged[j, :, i * width : (i + 1) * width] = terms[
                        i * PIECE : (i + 1) * PIECE
                    ].astype(staged.dtype)
                if cap % PIECE:
                    i = cap // PIECE
                    last = terms[i * PIECE : cap]
                    staged[j, :, i * width : end] = jnp.concatenate(
                        [last[:, : width // 2], last[:, width // 2 :]]
                    ).astype(staged.dtype)
                if j % part == part - 1:
                    some = pl.ds(j + 1 - part, part)
                    copies.append(
                        pltpu.make_async_copy(
                            staged.at[some, :, pl.ds(0, end)],
                            outs[k].at[some],
                            sems.at[j // part],
                        )
                    )
                    copies[-1].start()
            for c in copies:
                c.wait()


def up_terms(caps, way, select, low_mine, low_theirs, up_mine, up_theirs):
    chips, rank, width = up_mine.shape
    vmem = pl.BlockSpec(memory_space=pltpu.VMEM)
    shapes = [(chips, PIECE, cap * width // PIECE) for cap in caps]
    return pl.pallas_call(
        functools.partial(up_kernel, caps),
        in_specs=[pl.BlockSpec(memory_space=pltpu.SMEM)] + [vmem] * 5,
        out_specs=[pl.BlockSpec(memory_space=pl.ANY)] * len(caps),
        out_shape=[jax.ShapeDtypeStruct(shape, jnp.bfloat16) for shape in shapes],
        scratch_shapes=[
            pltpu.VMEM(shapes[-1], jnp.bfloat16),
            pltpu.SemaphoreType.DMA((2,)),
        ],
        compiler_params=pltpu.CompilerParams(vmem_limit_bytes=16 * 2**20),
        cost_estimate=pl.CostEstimate(
            flops=4 * caps[-1] * rank * chips * width,
            bytes_accessed=2 * (2 * rank + caps[-1]) * chips * width,
            transcendentals=0,
        ),
        name="up_terms",
    )(way, select, low_mine, low_theirs, up_mine, up_theirs)


def add_kernel(base, received, pick, pick_right, out):
    rows, width = base.shape
    line, total = received.shape
    whole, part = total // width, total % width
    step = width // 2
    for half in range(2):
        columns = slice(half * step, (half + 1) * step)
        value = base[:, columns]
        for i in range(whole):
            piece = received[:, i * width + half * step : i * width + (half + 1) * step]
            value += jnp.dot(
                pick[:, i * line : (i + 1) * line], piece, preferred_element_type=jnp.float32
            )
        if part:
            choice = pick_right[...] if half else pick[:, whole * line : (whole + 1) * line]
            value += jnp.dot(
                choice, received[:, whole * width :], preferred_element_type=jnp.float32
            )
        out[:, columns] = value.astype(out.dtype)


def add_received(base, received, pick, pick_right):
    rows, width = base.shape
    vmem = pl.BlockSpec(memory_space=pltpu.VMEM)
    return pl.pallas_call(
        add_kernel,
        in_specs=[vmem] * 4,
        out_specs=vmem,
        out_shape=jax.ShapeDtypeStruct((rows, width), jnp.bfloat16),
        compiler_params=pltpu.CompilerParams(vmem_limit_bytes=24 * 2**20),
        cost_estimate=pl.CostEstimate(
            flops=4 * pick.size * width, bytes_accessed=8 * rows * width, transcendentals=0
        ),
        name="add_received",
    )(base, received.reshape(-1, received.shape[2]), pick, pick_right)


def chip_pool(
    normed_input_rows,
    gate_base_weight,
    adapter_down_factors,
    adapter_up_factors,
    request_adapter_id,
    row_request,
    adapter_storage_slot,
):
    npool, chips = 16, 8
    member = lax.axis_index("pool")

    def swap(value, bits):
        return lax.ppermute(value, "pool", [(i, i ^ bits) for i in range(npool)])

    far = swap(normed_input_rows, 8)
    near = swap(normed_input_rows, 4)
    side = swap(normed_input_rows, 2)
    near, side = lax.optimization_barrier((near, side))
    side_across, far_near = swap(side, 12), swap(far, 4)
    across = swap(jnp.concatenate([near, far]), 2)
    half = jnp.concatenate(
        [normed_input_rows, far, near, side, side_across, across, far_near]
    )
    down, up = adapter_down_factors[0], adapter_up_factors[0]
    down_theirs = swap(down, 1)
    requests, rows = request_adapter_id.shape[0], row_request.shape[0]
    named = jnp.concatenate([row_request, request_adapter_id[:, 0], adapter_storage_slot])[None, :]
    select, way, up_mine, up_swapped = prepare(
        member, requests, named, up, chips, rows
    )
    up_theirs = swap(up_swapped, 1)

    half, up_theirs = lax.optimization_barrier((half, up_theirs))
    low_mine = low_values(half, down, down_theirs)
    low_theirs = swap(low_mine, 1)

    def exchange(terms):
        return lax.all_to_all(
            terms,
            "pool",
            split_axis=0,
            concat_axis=0,
            tiled=True,
            axis_index_groups=[[2 * i + c for i in range(chips)] for c in range(2)],
        )

    terms = up_terms(CHIP_CAPS, way, select, low_mine, low_theirs, up_mine, up_theirs)
    half, *terms = lax.optimization_barrier((half, *terms))

    def finish(k, half):
        received = exchange(terms[k])
        swapped, named_then = lax.optimization_barrier((swap(half, 1), named))
        pick, pick_right, order = picks(member, requests, named_then, chips, rows)
        x = jnp.concatenate([half, swapped])
        x = jnp.dot(order, x, preferred_element_type=jnp.float32).astype(jnp.bfloat16)
        base = jnp.dot(x, gate_base_weight, preferred_element_type=jnp.float32)
        base, received = lax.optimization_barrier((base, received))
        return add_received(base, received, pick, pick_right)

    ways = [functools.partial(finish, k) for k in range(len(CHIP_CAPS))]
    return lax.switch(way[0], ways, half)


def solution(mesh):
    in_specs = (
        P(("groups", "pool"), None),
        P(None, "pool"),
        P(("groups", "pool"), None, None),
        P(("groups", "pool"), None, None),
        P("groups", None),
        P("groups"),
        P("groups"),
    )
    out_specs = P("groups", "pool")

    def on_device(*blocks):
        width, share = blocks[1].shape[1], blocks[2].shape[0]
        chip_wise = mesh.shape["pool"] == 16 and width % 128 == 0 and share == 1
        return (chip_pool if chip_wise else any_pool)(*blocks)

    return jax.shard_map(
        on_device, mesh=mesh, in_specs=in_specs, out_specs=out_specs, check_vma=False
    )
```
